128 devices in a mesh: ctx: 16 (over z_hi, x, core), head: 8 (over z_lo, y).
Axes of the slice: x: 4, y: 4, z: 4 (z_hi: 2, z_lo: 2; z = z_hi * 2 + z_lo), core: 2. Of those that a mesh axis runs over, the one named last changes fastest.
Arguments:
- hidden_states: bfloat16 [16384, 4096], P('ctx'), may hold values from -6 to 6
- norm_gain: float32 [4096], replicated, may hold values from 0.5 to 2
- query_weight: bfloat16 [4096, 4096], P(None, 'head'), may hold values from -2 to 2
- key_weight: bfloat16 [4096, 1024], P(None, 'head'), may hold values from -2 to 2
- value_weight: bfloat16 [4096, 1024], P(None, 'head'), may hold values from -0.09375 to 0.09375
- output_weight: bfloat16 [4096, 4096], P('head'), may hold values from -0.09375 to 0.09375
- keep_flags: int32 [32], P('ctx'), may hold values from 0 to 1, as said below
- span_order: int32 [16], replicated, may hold values from 0 to 15, each once
Outputs:
- layer_output: bfloat16 [8192, 4096], P(('ctx', 'head'))
The draws below stay inside these ranges and needn't reach their ends.
Inputs may be any that keep to these rules, and one draw needn't show every extreme that they name: `keep_flags`: exactly 16 of the 32 spans are kept.
All inputs are finite; a program needn't handle non-finite values.
Results may differ from the reference program's by a relative error of at most 0.02.
The reference program's roundings to bfloat16 on the way count: a program that leaves them out, or rounds other values in their place, can miss the bound.
Values may be sent and summed in bfloat16 or wider, within the bound.
A program may use at most 128 MiB of HBM per device.

```python
import math
import jax
import jax.numpy as jnp
from jax import lax

D = 4096
HEADS = 32
KV_HEADS = 8
HEAD_DIM = 128
SPAN = 512
SPANS = 32
KEPT = 16
RAW = 16384
PIECE = 32
ROWS_DEV = 512
ROWS = 8192
N_CTX = 16
N_HEAD = 8


def query_base(key):
    return jax.random.normal(key, (D, HEADS * HEAD_DIM), jnp.float32) * D ** (-0.5)


def draw_query_weight(key, part):
    shared = query_base(key)
    return jnp.clip(shared, -2.0, 2.0).astype(jnp.bfloat16)


def draw_key_weight(key, part):
    key = jax.random.fold_in(key, 3)
    own_part = jax.random.normal(key, (D, KV_HEADS * HEAD_DIM), jnp.float32) * D ** (-0.5)
    return jnp.clip(own_part, -2.0, 2.0).astype(jnp.bfloat16)


def draw_keep_flags(key, part):
    key = jax.random.fold_in(key, 5)
    shuffled = jax.random.permutation(key, SPANS)
    return (shuffled < KEPT).astype(jnp.int32)


def levels(own_key, dims, split, low, top_value):
    def one(dim, parts):
        draws = jax.random.uniform(jax.random.fold_in(jax.random.fold_in(own_key, 6), dim), (parts,), jnp.float32, low / len(split), top_value / len(split))
        return jnp.repeat(jnp.exp(draws), dims[dim] // parts).reshape((-1,) + (1,) * (len(dims) - dim - 1))

    loudness = one(*split[0])
    for cut in split[1:]:
        loudness = loudness * one(*cut)
    return loudness


def noise(stream_key, dims, width, most, split=(), kind=jnp.bfloat16):
    values = jax.random.normal(stream_key, dims, jnp.float32) * width
    if len(split) > 0:
        values = levels(stream_key, dims, split, -0.22, 0.18) * values
    return jnp.clip(values, min=-most, max=most).astype(kind)


def setup_inputs(seed: int = 0) -> dict:
    splits = jax.random.split(jax.random.key(seed), 9)
    hidden_states = noise(splits[0], (RAW, D), 1.0, 6.0, ((0, 16),))
    norm_gain = jnp.clip(jnp.exp(jax.random.uniform(splits[1], (D,), jnp.float32, math.log(0.5), math.log(2.0))), 0.5, 2.0)
    query_weight = draw_query_weight(jax.random.fold_in(splits[8], 71), 0)
    key_weight = draw_key_weight(jax.random.fold_in(splits[8], 71), 0)
    value_weight = noise(splits[4], (D, KV_HEADS * HEAD_DIM), D ** -0.5, 0.09375, ((1, 8),))
    output_weight = noise(splits[5], (HEADS * HEAD_DIM, D), (HEADS * HEAD_DIM) ** -0.5, 0.09375, ((0, 8),))
    keep_flags = draw_keep_flags(jax.random.fold_in(splits[8], 71), 0)
    span_order = jax.random.permutation(splits[7], KEPT).astype(jnp.int32)
    return dict(hidden_states=hidden_states, norm_gain=norm_gain, query_weight=query_weight, key_weight=key_weight, value_weight=value_weight, output_weight=output_weight, keep_flags=keep_flags, span_order=span_order)


def rms_normed(activations, norm_gain):
    widened = activations.astype(jnp.float32)
    mean_square = lax.optimization_barrier(jnp.mean(widened * widened, axis=-1, keepdims=True))
    return (widened * lax.rsqrt(mean_square + 1e-05) * norm_gain.astype(jnp.float32)).astype(jnp.bfloat16)

def rotate(values, positions):
    half_width = HEAD_DIM // 2
    frequency = jnp.power(jnp.float32(500000.0), -2.0 * jnp.arange(half_width, dtype=jnp.float32) / HEAD_DIM)
    angles = positions.astype(jnp.float32)[:, None] * frequency[None, :]
    cosine = jnp.cos(angles)[:, None, :]
    sine_part = jnp.sin(angles)[:, None, :]
    shaped = values.reshape(values.shape[0], -1, HEAD_DIM)
    leading = shaped[..., :half_width]
    trailing = shaped[..., half_width:]
    turned = jnp.concatenate([leading * cosine - trailing * sine_part, trailing * cosine + leading * sine_part], axis=-1)
    return turned.reshape(values.shape)

def kept_positions(keep_flags, span_order):
    span_ids = jnp.nonzero(keep_flags, size=KEPT)[0].astype(jnp.int32)
    shifts = (span_order % N_CTX).astype(jnp.int32)
    rowids = jnp.arange(ROWS, dtype=jnp.int32)
    owner_device = rowids // ROWS_DEV
    within = rowids % ROWS_DEV // PIECE
    offset = rowids % PIECE
    return span_ids[within] * SPAN + (owner_device - shifts[within]) % N_CTX * PIECE + offset

def reference(hidden_states, norm_gain, query_weight, key_weight, value_weight, output_weight, keep_flags, span_order):
    normed = rms_normed(hidden_states, norm_gain)
    positions = kept_positions(keep_flags, span_order)
    gathered = normed[positions]
    query_states = rotate(jnp.dot(gathered, query_weight, preferred_element_type=jnp.float32), positions).astype(jnp.bfloat16)
    key_states = rotate(jnp.dot(gathered, key_weight, preferred_element_type=jnp.float32), positions).astype(jnp.bfloat16)
    value_states = jnp.dot(gathered, value_weight, preferred_element_type=jnp.float32).astype(jnp.bfloat16)
    group_size = HEADS // KV_HEADS
    per_head_q = query_states.reshape(ROWS, HEADS, HEAD_DIM).transpose(1, 0, 2)
    per_head_k = jnp.repeat(key_states.reshape(ROWS, KV_HEADS, HEAD_DIM).transpose(1, 0, 2), group_size, axis=0)
    per_head_v = jnp.repeat(value_states.reshape(ROWS, KV_HEADS, HEAD_DIM).transpose(1, 0, 2), group_size, axis=0)
    block_rows = math.gcd(ROWS, 1024)
    score_scale = 1.0 / math.sqrt(HEAD_DIM)

    def one_head(operands):
        head_q, head_k, head_v = operands

        def one_block(block_operands):
            query_block, query_pos = block_operands
            scores = jnp.dot(query_block, head_k.T, preferred_element_type=jnp.float32) * score_scale
            allowed = positions[None, :] <= query_pos[:, None]
            scores = jnp.where(allowed, scores, -1e+30)
            row_peak = lax.optimization_barrier(jnp.max(scores, axis=1, keepdims=True))
            expo = jnp.where(allowed, jnp.exp(scores - row_peak), 0.0)
            denominator = lax.optimization_barrier(jnp.sum(expo, axis=1, keepdims=True))
            mixture = jnp.dot(expo.astype(jnp.bfloat16), head_v, preferred_element_type=jnp.float32)
            return (mixture / denominator).astype(jnp.bfloat16)
        outputs = lax.map(one_block, (head_q.reshape(ROWS // block_rows, block_rows, HEAD_DIM), positions.reshape(ROWS // block_rows, block_rows)))
        return outputs.reshape(ROWS, HEAD_DIM)
    head_outputs = lax.map(one_head, (per_head_q, per_head_k, per_head_v))
    attended = head_outputs.transpose(1, 0, 2).reshape(ROWS, HEADS * HEAD_DIM)
    block_width = HEADS * HEAD_DIM // N_HEAD
    summed = jnp.zeros((ROWS, D), jnp.float32)
    for block_index in range(N_HEAD):
        block_term = jnp.dot(attended[:, block_index * block_width:(block_index + 1) * block_width], output_weight[block_index * block_width:(block_index + 1) * block_width], preferred_element_type=jnp.float32)
        rounded = lax.optimization_barrier(block_term.astype(jnp.bfloat16))
        summed = summed + rounded.astype(jnp.float32)
    return summed.astype(jnp.bfloat16)
```

```python
import functools
import math

import jax
import jax.numpy as jnp
import numpy as np
from jax import lax
from jax.experimental import pallas as pl
from jax.experimental.pallas import tpu as pltpu
from jax.sharding import PartitionSpec as P

MESH = pl.DeviceIdType.MESH
HEAD_DIM = 128
PIECE = 32
KEPT = 16
SPAN = 512
N_CTX = 16
LOG2E = math.log2(math.e)
F32 = jnp.float32
BF16 = jnp.bfloat16


def rope_tables():
    frequency = 500000.0 ** (-2.0 * np.arange(64, dtype=np.float64) / HEAD_DIM)
    frequency = np.concatenate([frequency, frequency])[None, :]
    sign = np.concatenate([-np.ones(64), np.ones(64)])[None, :]
    pieces = np.arange(N_CTX * 2 * SPAN // PIECE, dtype=np.float64)[:, None] * PIECE * frequency
    rows = np.arange(PIECE, dtype=np.float64)[:, None] * frequency
    base = np.stack([np.cos(pieces), np.sin(pieces)]).reshape(2, N_CTX, 32, 1, HEAD_DIM)
    inner = np.stack([np.cos(rows), np.sin(rows), np.cos(rows) * sign, np.sin(rows) * sign])
    return base.transpose(1, 2, 0, 3, 4).astype(np.float32), inner.astype(np.float32)


def kernel(
    hidden_hbm, gain_ref, wq_hbm, wk_hbm, wv_hbm, wo_hbm, flags_ref, order_ref, base_hbm, inner_ref,
    out_ref,
    hidden, wqkv, wo, wo_a, wo_b, base, normed, flag_src, flag_all, flag_sm, stage, recv,
    queries, kv, acc, peak, att, att_a, att_b, part_a, part_b, got_a, got_b, mine, zsend, zgot,
    load_sem, flag_send, flag_recv, a2a_send, a2a_recv, kv_send, kv_recv, w_send, w_recv, wc_send, wc_recv,
    att_send, att_recv, part_send, part_recv, z_send, z_recv, local_sem,
):
    me = lax.axis_index("ctx")
    head = lax.axis_index("head")
    zh, x, core = me // 8, (me // 2) % 4, me % 2
    zl, y = head // 4, head % 4
    pa = y + 1 - 2 * (y % 2)
    pb = 3 - y

    def ctx_at(dz, dx, dc):
        return ((zh + dz) % 2) * 8 + ((x + dx) % 4) * 2 + (core + dc) % 2

    def send(src, dst, ssem, rsem, ctx=None, hd=None):
        copy = pltpu.make_async_remote_copy(
            src_ref=src, dst_ref=dst, send_sem=ssem, recv_sem=rsem,
            device_id=(me if ctx is None else ctx, head if hd is None else hd),
            device_id_type=MESH,
        )
        copy.start()
        return copy

    def await_recv(dst, rsem):
        pltpu.make_async_remote_copy(
            src_ref=dst, dst_ref=dst, send_sem=rsem, recv_sem=rsem,
            device_id=(me, head), device_id_type=MESH,
        ).wait_recv()

    sends = []

    loads = []

    def load(src, dst):
        copy = pltpu.make_async_copy(src, dst, load_sem.at[len(loads)])
        copy.start()
        loads.append(copy)
        return copy

    load_base = load(base_hbm.at[me], base)
    load_hidden = load(hidden_hbm, hidden)
    load_q = load(wq_hbm, wqkv.at[:, pl.ds(0, 512)])
    load_k = load(wk_hbm, wqkv.at[:, pl.ds(512, 128)])
    load_v = load(wv_hbm, wqkv.at[:, pl.ds(640, 128)])
    load_o = load(wo_hbm, wo)

    barrier = pltpu.get_barrier_semaphore()
    for i in range(1, N_CTX):
        pl.semaphore_signal(barrier, inc=1, device_id=((me + i) % N_CTX, head), device_id_type=MESH)
    for hd in (zl * 4 + pa, zl * 4 + pb, (1 - zl) * 4 + y):
        pl.semaphore_signal(barrier, inc=1, device_id=(me, hd), device_id_type=MESH)
    pl.semaphore_wait(barrier, N_CTX - 1 + 3)

    lane = lax.broadcasted_iota(jnp.int32, (1, 128), 1)
    own_flags = jnp.where(lane == 0, flags_ref[0], jnp.where(lane == 1, flags_ref[1], 0))
    flag_src[...] = own_flags
    flag_all[me] = own_flags
    for i in range(1, N_CTX):
        sends.append(send(flag_src, flag_all.at[me], flag_send.at[i], flag_recv.at[me], ctx=(me + i) % N_CTX))
    for i in range(1, N_CTX):
        src = (me + i) % N_CTX
        await_recv(flag_all.at[src], flag_recv.at[src])
    to_scalars = pltpu.make_async_copy(flag_all, flag_sm, local_sem)
    to_scalars.start()
    to_scalars.wait()

    first_rank = jnp.int32(0)
    for i in range(N_CTX):
        first_rank += jnp.where(i < me, flag_sm[i, 0, 0] + flag_sm[i, 0, 1], 0)

    def shift_of(rank):
        return order_ref[rank] % N_CTX

    slot_span = (1 - flag_sm[me, 0, 0], jnp.int32(1))
    slot_shift = (shift_of(jnp.minimum(first_rank, KEPT - 1)), shift_of(jnp.minimum(first_rank + 1, KEPT - 1)))

    load_base.wait()
    load_hidden.wait()

    load_o.wait()
    half = pl.ds(core * 256, 256)
    other_half = pl.ds((1 - core) * 256, 256)
    cols_a, cols_b = pl.ds(0, 2048), pl.ds(2048, 2048)
    sends.append(send(wo.at[half, cols_a], wo_a.at[half, :], w_send.at[0], w_recv.at[0], hd=zl * 4 + pa))
    sends.append(send(wo.at[half, cols_b], wo_b.at[half, :], w_send.at[1], w_recv.at[1], hd=zl * 4 + pb))

    load_q.wait()
    load_k.wait()
    load_v.wait()

    def project_chunk(chunk, _):
        dx = (chunk + 1) % 4
        targets = [ctx_at(dz, dx, dc) for dz in (1, 0) for dc in (1, 0)]
        for slot in range(2):
            def norm_piece(i, _):
                target = ctx_at(1 - i // 2, dx, 1 - i % 2)
                piece = slot_span[slot] * 16 + (target + N_CTX - slot_shift[slot]) % N_CTX
                total = jnp.zeros((PIECE, 128), F32)
                for c in range(0, 4096, 512):
                    part = hidden[piece, :, c:c + 512].astype(F32)
                    part = part * part
                    total += (part[:, :128] + part[:, 128:256]) + (part[:, 256:384] + part[:, 384:])
                scale = lax.rsqrt(jnp.sum(total, axis=1, keepdims=True) * (1.0 / 4096) + 1e-05)
                dst = pl.ds(pl.multiple_of(i * 64 + slot * PIECE, PIECE), PIECE)
                for c in range(0, 4096, 512):
                    part = hidden[piece, :, c:c + 512].astype(F32)
                    normed[dst, c:c + 512] = (part * scale * gain_ref[:, c:c + 512]).astype(BF16)
                return 0
            lax.fori_loop(0, 4, norm_piece, 0)
        projected = jnp.dot(normed[...], wqkv[...], preferred_element_type=F32)
        for i, target in enumerate(targets):
            for slot in range(2):
                piece = slot_span[slot] * 16 + (target + N_CTX - slot_shift[slot]) % N_CTX
                cos_base, sin_base = base[piece, 0], base[piece, 1]
                cosine = cos_base * inner_ref[0] - sin_base * inner_ref[1]
                sine = sin_base * inner_ref[2] + cos_base * inner_ref[3]
                lo = i * 64 + slot * PIECE
                for part in range(6):
                    block = projected[lo:lo + PIECE, part * 128:(part + 1) * 128]
                    if part < 5:
                        block = block * cosine + pltpu.roll(block, 64, 1) * sine
                    stage[target, slot, part] = block.astype(BF16)
            if i < 3:
                send(stage.at[target], recv.at[me], a2a_send.at[target], a2a_recv.at[me], ctx=target)
            else:
                @pl.when(chunk < 3)
                def _():
                    send(stage.at[target], recv.at[me], a2a_send.at[target], a2a_recv.at[me], ctx=target)
        return 0

    lax.fori_loop(0, 4, project_chunk, 0)
    own = pltpu.make_async_copy(stage.at[me], recv.at[me], local_sem)
    own.start()

    arrival = [jnp.int32(0)] * KEPT
    rank = jnp.int32(0)
    for i in range(N_CTX):
        f0, f1 = flag_sm[i, 0, 0], flag_sm[i, 0, 1]
        for flag, place in ((f0, 2 * i), (f1, 2 * i + f0)):
            for r in range(KEPT):
                arrival[r] = jnp.where((flag == 1) & (rank == r), place, arrival[r])
            rank = rank + flag
    own.wait()
    for i in range(1, N_CTX):
        src = (me + i) % N_CTX
        await_recv(recv.at[src], a2a_recv.at[src])

    for r in range(KEPT):
        src, slot = arrival[r] // 2, arrival[r] % 2
        for part in range(4):
            queries[r * 128 + part * 32:r * 128 + part * 32 + 32, :] = recv[src, slot, part]
        rows = slice((r % 4) * 32, (r % 4) * 32 + 32)
        kv[r // 4, me, 0, rows, :] = recv[src, slot, 4]
        kv[r // 4, me, 1, rows, :] = recv[src, slot, 5]

    sibling = ctx_at(0, 0, 1)
    zmate = ctx_at(1, 0, 0)
    xplus, xminus = ctx_at(0, 1, 0), ctx_at(0, 3, 0)

    def pass_on(q, src, way, target):
        sends.append(send(kv.at[q, src], kv.at[q, src], kv_send.at[q, src, way], kv_recv.at[q, src], ctx=target))

    def arrived(q, src):
        await_recv(kv.at[q, src], kv_recv.at[q, src])

    for q in range(4):
        pass_on(q, me, 0, zmate)
    for q in range(4):
        pass_on(q, me, 1, xplus)
        pass_on(q, me, 2, xminus)
        pass_on(q, me, 3, sibling)
        arrived(q, zmate)
        pass_on(q, zmate, 1, xplus)
        pass_on(q, zmate, 2, xminus)
        pass_on(q, zmate, 3, sibling)
    for q in range(4):
        for dz in range(2):
            arrived(q, ctx_at(dz, 3, 0))
            if dz == 0:
                pass_on(q, ctx_at(dz, 3, 0), 1, xplus)
            pass_on(q, ctx_at(dz, 3, 0), 3, sibling)
            arrived(q, ctx_at(dz, 1, 0))
            if dz == 1:
                pass_on(q, ctx_at(dz, 1, 0), 2, xminus)
            pass_on(q, ctx_at(dz, 1, 0), 3, sibling)
    for q in range(4):
        for dz in range(2):
            arrived(q, ctx_at(dz, 2, 0))
            pass_on(q, ctx_at(dz, 2, 0), 3, sibling)
    await_recv(wo_a.at[half, :], w_recv.at[0])
    await_recv(wo_b.at[half, :], w_recv.at[1])
    sends.append(send(wo_a.at[half, :], wo_a.at[half, :], wc_send.at[0], wc_recv.at[0], ctx=sibling))
    sends.append(send(wo_b.at[half, :], wo_b.at[half, :], wc_send.at[1], wc_recv.at[1], ctx=sibling))
    for q in range(4):
        for dz in range(2):
            for dx in range(4):
                arrived(q, ctx_at(dz, dx, 1))

    factor = LOG2E / math.sqrt(HEAD_DIM)
    ones = jnp.ones((2048, 128), BF16)
    rows_block = 128
    key_lane = lax.broadcasted_iota(jnp.int32, (1, 2048), 1)

    def attend(g, q, masked):
        keys = kv[q, :, 0].reshape(2048, 128)
        values = jnp.concatenate([kv[q, :, 1].reshape(2048, 128), ones], axis=1)
        if masked:
            key_pos = jnp.zeros((1, 2048), jnp.int32)
            for b in range(4):
                place = (key_lane // 128 + N_CTX - shift_of(4 * q + b)) % N_CTX
                here = (key_lane % 128) // 32 == b
                key_pos = jnp.where(here, (4 * q + b) * SPAN + place * PIECE + key_lane % PIECE, key_pos)

        def block(a, _):
            rows = pl.ds(pl.multiple_of(g * 512 + a * rows_block, rows_block), rows_block)
            scores = lax.dot_general(queries[rows, :], keys, (((1,), (1,)), ((), ())), preferred_element_type=F32)
            if masked:
                r = 4 * g + a
                row = lax.broadcasted_iota(jnp.int32, (rows_block, 1), 0) % PIECE
                query_pos = r * SPAN + ((me + N_CTX - shift_of(r)) % N_CTX) * PIECE + row
                scores = jnp.where(key_pos <= query_pos, scores, -1e30)
            top = jnp.max(scores, axis=1, keepdims=True)
            if q == 0:
                new_peak = jnp.broadcast_to(top, (rows_block, 128))
            else:
                old = peak[rows, :]
                new_peak = jnp.maximum(old, top)
            expo = jnp.exp2((scores - new_peak[:, :1]) * factor).astype(BF16)
            mixed = jnp.dot(expo, values, preferred_element_type=F32)
            if q == 0:
                acc[rows, :] = mixed
            else:
                fade = jnp.exp2((old - new_peak) * factor)
                acc[rows, :] = acc[rows, :] * jnp.concatenate([fade, fade], axis=1) + mixed
            peak[rows, :] = new_peak
            return 0

        lax.fori_loop(0, 512 // rows_block, block, 0)

    for q in range(4):
        attend(q, q, True)
        if q < 3:
            def later(g, _, q=q):
                attend(g, q, False)
                return 0
            lax.fori_loop(q + 1, 4, later, 0)

    for r in range(KEPT):
        hd = r // 2
        for part in range(4):
            rows = slice(r * 128 + part * 32, r * 128 + part * 32 + 32)
            value = (acc[rows, :128] / acc[rows, 128:]).astype(BF16)
            att[hd % 4, hd // 4, (r % 2) * 32:(r % 2) * 32 + 32, part * 128:(part + 1) * 128] = value

    far = (y + 2) % 4
    at_pa, at_pb, at_z = zl * 4 + pa, zl * 4 + pb, (1 - zl) * 4 + y
    sends.append(send(att.at[far], att_a.at[1], att_send.at[0], att_recv.at[0], hd=at_pa))
    sends.append(send(att.at[far], att_b.at[1], att_send.at[1], att_recv.at[1], hd=at_pb))
    sends.append(send(att.at[pa], att_a.at[0], att_send.at[2], att_recv.at[2], hd=at_pa))
    sends.append(send(att.at[pb], att_b.at[0], att_send.at[3], att_recv.at[3], hd=at_pb))
    await_recv(wo_a.at[other_half, :], wc_recv.at[0])
    await_recv(wo_b.at[other_half, :], wc_recv.at[1])

    def term(rows_ref, weights):
        flat = rows_ref.reshape(128, 512)
        return jnp.dot(flat, weights, preferred_element_type=F32).astype(BF16).astype(F32)

    width = 512
    steps = 2048 // width
    await_recv(att_a.at[1], att_recv.at[0])
    await_recv(att_b.at[1], att_recv.at[1])

    def far_step(c, _):
        cols = pl.ds(pl.multiple_of(c * width, width), width)
        cols_far = pl.ds(pl.multiple_of(2048 + c * width, width), width)
        total = term(att[pb], wo[:, cols]) + term(att_a[1], wo_a[:, cols])
        part_a[c] = total.astype(BF16)
        send(part_a.at[c], got_a.at[c], part_send.at[0, c], part_recv.at[0, c], hd=at_pb)
        total = term(att[pa], wo[:, cols_far]) + term(att_b[1], wo_b[:, cols])
        part_b[c] = total.astype(BF16)
        send(part_b.at[c], got_b.at[c], part_send.at[1, c], part_recv.at[1, c], hd=at_pa)
        return 0

    lax.fori_loop(0, steps, far_step, 0)
    await_recv(att_a.at[0], att_recv.at[2])
    await_recv(att_b.at[0], att_recv.at[3])

    def near_step(c, _):
        cols = pl.ds(pl.multiple_of(c * width, width), width)
        cols_far = pl.ds(pl.multiple_of(2048 + c * width, width), width)
        mine[c] = term(att[y], wo[:, cols]) + term(att_a[0], wo_a[:, cols])
        mine[steps + c] = term(att[y], wo[:, cols_far]) + term(att_b[0], wo_b[:, cols])
        return 0

    lax.fori_loop(0, steps, near_step, 0)

    z_rows = pl.ds(pl.multiple_of((1 - zl) * 64, 64), 64)
    own_rows = pl.ds(pl.multiple_of(zl * 64, 64), 64)

    def sum_step(c, _):
        for side, got in ((0, got_a), (1, got_b)):
            slot = side * steps + c
            await_recv(got.at[c], part_recv.at[side, c])
            mine[slot] = mine[slot] + got[c].astype(F32)
            zsend[slot] = mine[slot, z_rows, :].astype(BF16)
            send(zsend.at[slot], zgot.at[slot], z_send.at[slot], z_recv.at[slot], hd=at_z)
        return 0

    lax.fori_loop(0, steps, sum_step, 0)

    def final_step(slot, _):
        await_recv(zgot.at[slot], z_recv.at[slot])
        cols = pl.ds(pl.multiple_of(slot * width, width), width)
        out_ref[:, cols] = (mine[slot, own_rows, :] + zgot[slot].astype(F32)).astype(BF16)
        return 0

    lax.fori_loop(0, 2 * steps, final_step, 0)

    for copy in sends:
        copy.wait_send()

    def await_send(src, ssem):
        pltpu.make_async_remote_copy(
            src_ref=src, dst_ref=src, send_sem=ssem, recv_sem=ssem,
            device_id=(me, head), device_id_type=MESH,
        ).wait_send()

    for i in range(1, N_CTX):
        target = (me + i) % N_CTX
        await_send(stage.at[target], a2a_send.at[target])

    def drain(c, _):
        await_send(part_a.at[c], part_send.at[0, c])
        await_send(part_b.at[c], part_send.at[1, c])
        await_send(zsend.at[c], z_send.at[c])
        await_send(zsend.at[steps + c], z_send.at[steps + c])
        return 0

    lax.fori_loop(0, steps, drain, 0)


def body(hidden_states, norm_gain, query_weight, key_weight, value_weight, output_weight, keep_flags, span_order):
    base, inner = rope_tables()
    vmem = pl.BlockSpec(memory_space=pltpu.VMEM)
    smem = pl.BlockSpec(memory_space=pltpu.SMEM)
    anywhere = pl.BlockSpec(memory_space=pl.ANY)
    dma = pltpu.SemaphoreType.DMA
    return pl.pallas_call(
        kernel,
        out_shape=jax.ShapeDtypeStruct((64, 4096), BF16),
        in_specs=[anywhere, vmem, anywhere, anywhere, anywhere, anywhere, smem, smem, anywhere, vmem],
        out_specs=vmem,
        scratch_shapes=[
            pltpu.VMEM((32, 32, 4096), BF16),
            pltpu.VMEM((4096, 768), BF16),
            pltpu.VMEM((512, 4096), BF16),
            pltpu.VMEM((512, 2048), BF16),
            pltpu.VMEM((512, 2048), BF16),
            pltpu.VMEM((32, 2, 1, 128), F32),
            pltpu.VMEM((256, 4096), BF16),
            pltpu.VMEM((1, 128), jnp.int32),
            pltpu.VMEM((16, 1, 128), jnp.int32),
            pltpu.SMEM((16, 1, 128), jnp.int32),
            pltpu.VMEM((16, 2, 6, 32, 128), BF16),
            pltpu.VMEM((16, 2, 6, 32, 128), BF16),
            pltpu.VMEM((2048, 128), BF16),
            pltpu.VMEM((4, 16, 2, 128, 128), BF16),
            pltpu.VMEM((2048, 256), F32),
            pltpu.VMEM((2048, 128), F32),
            pltpu.VMEM((4, 2, 64, 512), BF16),
            pltpu.VMEM((2, 2, 64, 512), BF16),
            pltpu.VMEM((2, 2, 64, 512), BF16),
            pltpu.VMEM((4, 128, 512), BF16),
            pltpu.VMEM((4, 128, 512), BF16),
            pltpu.VMEM((4, 128, 512), BF16),
            pltpu.VMEM((4, 128, 512), BF16),
            pltpu.VMEM((8, 128, 512), F32),
            pltpu.VMEM((8, 64, 512), BF16),
            pltpu.VMEM((8, 64, 512), BF16),
            dma((8,)),
            dma((16,)), dma((16,)),
            dma((16,)), dma((16,)),
            dma((4, 16, 4)), dma((4, 16)),
            dma((2,)), dma((2,)), dma((2,)), dma((2,)),
            dma((4,)), dma((4,)),
            dma((2, 4)), dma((2, 4)),
            dma((8,)), dma((8,)),
            dma,
        ],
        compiler_params=pltpu.CompilerParams(
            collective_id=1, has_side_effects=True, vmem_limit_bytes=60 * 2**20
        ),
        name="prefill",
    )(
        hidden_states.reshape(32, 32, 4096), norm_gain.reshape(1, 4096), query_weight, key_weight, value_weight, output_weight,
        keep_flags, span_order, jnp.asarray(base), jnp.asarray(inner),
    )


def solution(mesh):
    return jax.shard_map(
        body,
        mesh=mesh,
        in_specs=(
            P("ctx", None),
            P(),
            P(None, "head"),
            P(None, "head"),
            P(None, "head"),
            P("head", None),
            P("ctx"),
            P(),
        ),
        out_specs=P(("ctx", "head"), None),
        check_vma=False,
    )
```

```python
import functools
import math

import jax
import jax.numpy as jnp
import numpy as np
from jax import lax
from jax.experimental import pallas as pl
from jax.experimental.pallas import tpu as pltpu
from jax.sharding import PartitionSpec as P

MESH = pl.DeviceIdType.MESH
HEAD_DIM = 128
PIECE = 32
KEPT = 16
SPAN = 512
N_CTX = 16
LOG2E = math.log2(math.e)
F32 = jnp.float32
BF16 = jnp.bfloat16


def rope_tables():
    frequency = 500000.0 ** (-2.0 * np.arange(64, dtype=np.float64) / HEAD_DIM)
    frequency = np.concatenate([frequency, frequency])[None, :]
    sign = np.concatenate([-np.ones(64), np.ones(64)])[None, :]
    pieces = np.arange(N_CTX * 2 * SPAN // PIECE, dtype=np.float64)[:, None] * PIECE * frequency
    rows = np.arange(PIECE, dtype=np.float64)[:, None] * frequency
    base = np.stack([np.cos(pieces), np.sin(pieces)]).reshape(2, N_CTX, 32, 1, HEAD_DIM)
    inner = np.stack([np.cos(rows), np.sin(rows), np.cos(rows) * sign, np.sin(rows) * sign])
    return base.transpose(1, 2, 0, 3, 4).astype(np.float32), inner.astype(np.float32)


def kernel(
    hidden_hbm, gain_ref, wq_hbm, wk_hbm, wv_hbm, wo_hbm, flags_ref, order_ref, base_hbm, inner_ref,
    out_ref,
    hidden, wqkv, wo, wo_a, wo_b, base, normed, flag_src, flag_all, flag_sm, stage, recv,
    queries, kv, acc, peak, att, att_a, att_b, part_a, part_b, got_a, got_b, mine, zsend, zgot,
    load_sem, flag_send, flag_recv, a2a_send, a2a_recv, kv_send, kv_recv, w_send, w_recv, wc_send, wc_recv,
    att_send, att_recv, part_send, part_recv, z_send, z_recv, local_sem,
):
    me = lax.axis_index("ctx")
    head = lax.axis_index("head")
    zh, x, core = me // 8, (me // 2) % 4, me % 2
    zl, y = head // 4, head % 4
    pa = y + 1 - 2 * (y % 2)
    pb = 3 - y

    def ctx_at(dz, dx, dc):
        return ((zh + dz) % 2) * 8 + ((x + dx) % 4) * 2 + (core + dc) % 2

    def send(src, dst, ssem, rsem, ctx=None, hd=None):
        copy = pltpu.make_async_remote_copy(
            src_ref=src, dst_ref=dst, send_sem=ssem, recv_sem=rsem,
            device_id=(me if ctx is None else ctx, head if hd is None else hd),
            device_id_type=MESH,
        )
        copy.start()
        return copy

    def await_recv(dst, rsem):
        pltpu.make_async_remote_copy(
            src_ref=dst, dst_ref=dst, send_sem=rsem, recv_sem=rsem,
            device_id=(me, head), device_id_type=MESH,
        ).wait_recv()

    sends = []

    loads = []

    def load(src, dst):
        copy = pltpu.make_async_copy(src, dst, load_sem.at[len(loads)])
        copy.start()
        loads.append(copy)
        return copy

    load_base = load(base_hbm.at[me], base)
    load_hidden = load(hidden_hbm, hidden)
    load_q = load(wq_hbm, wqkv.at[:, pl.ds(0, 512)])
    load_k = load(wk_hbm, wqkv.at[:, pl.ds(512, 128)])
    load_v = load(wv_hbm, wqkv.at[:, pl.ds(640, 128)])
    load_o = load(wo_hbm, wo)

    barrier = pltpu.get_barrier_semaphore()
    for i in range(1, N_CTX):
        pl.semaphore_signal(barrier, inc=1, device_id=((me + i) % N_CTX, head), device_id_type=MESH)
    for hd in (zl * 4 + pa, zl * 4 + pb, (1 - zl) * 4 + y):
        pl.semaphore_signal(barrier, inc=1, device_id=(me, hd), device_id_type=MESH)
    pl.semaphore_wait(barrier, N_CTX - 1 + 3)

    lane = lax.broadcasted_iota(jnp.int32, (1, 128), 1)
    own_flags = jnp.where(lane == 0, flags_ref[0], jnp.where(lane == 1, flags_ref[1], 0))
    flag_src[...] = own_flags
    flag_all[me] = own_flags
    for i in range(1, N_CTX):
        sends.append(send(flag_src, flag_all.at[me], flag_send.at[i], flag_recv.at[me], ctx=(me + i) % N_CTX))
    for i in range(1, N_CTX):
        src = (me + i) % N_CTX
        await_recv(flag_all.at[src], flag_recv.at[src])
    to_scalars = pltpu.make_async_copy(flag_all, flag_sm, local_sem)
    to_scalars.start()
    to_scalars.wait()

    first_rank = jnp.int32(0)
    for i in range(N_CTX):
        first_rank += jnp.where(i < me, flag_sm[i, 0, 0] + flag_sm[i, 0, 1], 0)

    def shift_of(rank):
        return order_ref[rank] % N_CTX

    slot_span = (1 - flag_sm[me, 0, 0], jnp.int32(1))
    slot_shift = (shift_of(jnp.minimum(first_rank, KEPT - 1)), shift_of(jnp.minimum(first_rank + 1, KEPT - 1)))

    load_base.wait()
    load_hidden.wait()

    load_o.wait()
    half = pl.ds(core * 256, 256)
    other_half = pl.ds((1 - core) * 256, 256)
    cols_a, cols_b = pl.ds(0, 2048), pl.ds(2048, 2048)
    sends.append(send(wo.at[half, cols_a], wo_a.at[half, :], w_send.at[0], w_recv.at[0], hd=zl * 4 + pa))
    sends.append(send(wo.at[half, cols_b], wo_b.at[half, :], w_send.at[1], w_recv.at[1], hd=zl * 4 + pb))

    load_q.wait()
    load_k.wait()
    load_v.wait()

    def project_chunk(chunk, _):
        dx = (chunk + 1) % 4
        targets = [ctx_at(dz, dx, dc) for dz in (1, 0) for dc in (1, 0)]
        for slot in range(2):
            def norm_piece(i, _):
                target = ctx_at(1 - i // 2, dx, 1 - i % 2)
                piece = slot_span[slot] * 16 + (target + N_CTX - slot_shift[slot]) % N_CTX
                total = jnp.zeros((PIECE, 128), F32)
                for c in range(0, 4096, 512):
                    part = hidden[piece, :, c:c + 512].astype(F32)
                    part = part * part
                    total += (part[:, :128] + part[:, 128:256]) + (part[:, 256:384] + part[:, 384:])
                scale = lax.rsqrt(jnp.sum(total, axis=1, keepdims=True) * (1.0 / 4096) + 1e-05)
                dst = pl.ds(pl.multiple_of(i * 64 + slot * PIECE, PIECE), PIECE)
                for c in range(0, 4096, 512):
                    part = hidden[piece, :, c:c + 512].astype(F32)
                    normed[dst, c:c + 512] = (part * scale * gain_ref[:, c:c + 512]).astype(BF16)
                return 0
            lax.fori_loop(0, 4, norm_piece, 0)
        projected = jnp.dot(normed[...], wqkv[...], preferred_element_type=F32)
        for i, target in enumerate(targets):
            for slot in range(2):
                piece = slot_span[slot] * 16 + (target + N_CTX - slot_shift[slot]) % N_CTX
                cos_base, sin_base = base[piece, 0], base[piece, 1]
                cosine = cos_base * inner_ref[0] - sin_base * inner_ref[1]
                sine = sin_base * inner_ref[2] + cos_base * inner_ref[3]
                lo = i * 64 + slot * PIECE
                for part in range(6):
                    block = projected[lo:lo + PIECE, part * 128:(part + 1) * 128]
                    if part < 5:
                        block = block * cosine + pltpu.roll(block, 64, 1) * sine
                    stage[target, slot, part] = block.astype(BF16)
            if i < 3:
                send(stage.at[target], recv.at[me], a2a_send.at[target], a2a_recv.at[me], ctx=target)
            else:
                @pl.when(chunk < 3)
                def _():
                    send(stage.at[target], recv.at[me], a2a_send.at[target], a2a_recv.at[me], ctx=target)
        return 0

    lax.fori_loop(0, 4, project_chunk, 0)
    own = pltpu.make_async_copy(stage.at[me], recv.at[me], local_sem)
    own.start()

    arrival = [jnp.int32(0)] * KEPT
    rank = jnp.int32(0)
    for i in range(N_CTX):
        f0, f1 = flag_sm[i, 0, 0], flag_sm[i, 0, 1]
        for flag, place in ((f0, 2 * i), (f1, 2 * i + f0)):
            for r in range(KEPT):
                arrival[r] = jnp.where((flag == 1) & (rank == r), place, arrival[r])
            rank = rank + flag
    own.wait()
    for i in range(1, N_CTX):
        src = (me + i) % N_CTX
        await_recv(recv.at[src], a2a_recv.at[src])

    for r in range(KEPT):
        src, slot = arrival[r] // 2, arrival[r] % 2
        for part in range(4):
            queries[r * 128 + part * 32:r * 128 + part * 32 + 32, :] = recv[src, slot, part]
        rows = slice((r % 4) * 32, (r % 4) * 32 + 32)
        kv[r // 4, me, 0, rows, :] = recv[src, slot, 4]
        kv[r // 4, me, 1, rows, :] = recv[src, slot, 5]

    sibling = ctx_at(0, 0, 1)
    zmate = ctx_at(1, 0, 0)
    xplus, xminus = ctx_at(0, 1, 0), ctx_at(0, 3, 0)

    def pass_on(q, src, way, target):
        send(kv.at[q, src], kv.at[q, src], kv_send.at[q, src, way], kv_recv.at[q, src], ctx=target)

    def arrived(q, src):
        await_recv(kv.at[q, src], kv_recv.at[q, src])

    def gather_own(q):
        pass_on(q, me, 1, xplus)
        pass_on(q, me, 2, xminus)
        pass_on(q, me, 3, sibling)

    def gather_mate(q):
        arrived(q, zmate)
        pass_on(q, zmate, 1, xplus)
        pass_on(q, zmate, 2, xminus)
        pass_on(q, zmate, 3, sibling)

    def gather_near(q):
        for dz in range(2):
            left, right = ctx_at(dz, 3, 0), ctx_at(dz, 1, 0)
            arrived(q, left)
            if dz == 0:
                pass_on(q, left, 1, xplus)
            pass_on(q, left, 3, sibling)
            arrived(q, right)
            if dz == 1:
                pass_on(q, right, 2, xminus)
            pass_on(q, right, 3, sibling)

    def gather_far(q):
        for dz in range(2):
            across = ctx_at(dz, 2, 0)
            arrived(q, across)
            pass_on(q, across, 3, sibling)

    def gather_end(q):
        for dz in range(2):
            for dx in range(4):
                arrived(q, ctx_at(dz, dx, 1))

    factor = LOG2E / math.sqrt(HEAD_DIM)
    block_rows = 128
    blocks = 512 // block_rows

    def attend(g, q, masked):
        keys = kv[q, :, 0].reshape(2048, 128)
        values = jnp.concatenate([kv[q, :, 1].reshape(2048, 128), jnp.ones((2048, 128), BF16)], axis=1)
        if masked:
            key_lane = lax.broadcasted_iota(jnp.int32, (1, 2048), 1)
            key_pos = jnp.zeros((1, 2048), jnp.int32)
            for b in range(4):
                place = (key_lane // 128 + N_CTX - shift_of(4 * q + b)) % N_CTX
                here = (key_lane % 128) // 32 == b
                key_pos = jnp.where(here, b * SPAN + place * PIECE + key_lane % PIECE, key_pos)

        def rows_of(a):
            return pl.ds(pl.multiple_of(g * 512 + a * block_rows, block_rows), block_rows)

        def score(a):
            return lax.dot_general(
                queries[rows_of(a), :], keys, (((1,), (1,)), ((), ())), preferred_element_type=F32
            )

        scores = score(0)
        for a in range(blocks):
            rows = rows_of(a)
            coming = score(a + 1) if a + 1 < blocks else None
            if masked:
                row = lax.broadcasted_iota(jnp.int32, (block_rows, 1), 0) % PIECE
                query_pos = a * SPAN + ((me + N_CTX - shift_of(4 * q + a)) % N_CTX) * PIECE + row
                scores = jnp.where(key_pos <= query_pos, scores, -1e30)
            old = peak[rows, :]
            new = jnp.maximum(old, jnp.max(scores, axis=1, keepdims=True))
            peak[rows, :] = new
            expo = jnp.exp2((scores - new[:, :1]) * factor).astype(BF16)
            fade = jnp.exp2((old - new) * factor)
            mixed = jnp.dot(expo, values, preferred_element_type=F32)
            acc[rows, :] = acc[rows, :] * jnp.concatenate([fade, fade], axis=1) + mixed
            scores = coming

    def finish(g):
        for r in range(4 * g, 4 * g + 4):
            hd = r // 2
            for part in range(4):
                rows = slice(r * 128 + part * 32, r * 128 + part * 32 + 32)
                value = (acc[rows, :128] / acc[rows, 128:]).astype(BF16)
                att[hd % 4, hd // 4, (r % 2) * 32:(r % 2) * 32 + 32, part * 128:(part + 1) * 128] = value

    far = (y + 2) % 4
    at_pa, at_pb, at_z = zl * 4 + pa, zl * 4 + pb, (1 - zl) * 4 + y
    att_moves = ((far, att_a, 1, at_pa), (far, att_b, 1, at_pb), (pa, att_a, 0, at_pa), (pb, att_b, 0, at_pb))

    def exchange(z):
        for i, (block, dst, slot, hd) in enumerate(att_moves):
            send(att.at[block, z], dst.at[slot, z], att_send.at[z, i], att_recv.at[z, i], hd=hd)

    def term(rows, weights):
        return jnp.dot(rows, weights, preferred_element_type=F32).astype(BF16).astype(F32)

    width = 512
    steps = 2048 // width

    def two_cols(c):
        return (
            pl.ds(pl.multiple_of(c * width, width), width),
            pl.ds(pl.multiple_of(2048 + c * width, width), width),
        )

    def project_far(z):
        await_recv(att_a.at[1, z], att_recv.at[z, 0])
        await_recv(att_b.at[1, z], att_recv.at[z, 1])

        def step(c, _):
            cols, cols_b = two_cols(c)
            total = term(att[pb, z], wo[:, cols]) + term(att_a[1, z], wo_a[:, cols])
            part_a[z, c] = total.astype(BF16)
            send(part_a.at[z, c], got_a.at[z, c], part_send.at[z, 0, c], part_recv.at[z, 0, c], hd=at_pb)
            total = term(att[pa, z], wo[:, cols_b]) + term(att_b[1, z], wo_b[:, cols])
            part_b[z, c] = total.astype(BF16)
            send(part_b.at[z, c], got_b.at[z, c], part_send.at[z, 1, c], part_recv.at[z, 1, c], hd=at_pa)
            return 0

        lax.fori_loop(0, steps, step, 0)

    def project_near(z):
        await_recv(att_a.at[0, z], att_recv.at[z, 2])
        await_recv(att_b.at[0, z], att_recv.at[z, 3])

        def step(c, _):
            cols, cols_b = two_cols(c)
            mine[z, c] = term(att[y, z], wo[:, cols]) + term(att_a[0, z], wo_a[:, cols])
            mine[z, steps + c] = term(att[y, z], wo[:, cols_b]) + term(att_b[0, z], wo_b[:, cols])
            return 0

        lax.fori_loop(0, steps, step, 0)

    def sum_up(z):
        def step(c, _):
            for side, got in ((0, got_a), (1, got_b)):
                slot = side * steps + c
                await_recv(got.at[z, c], part_recv.at[z, side, c])
                total = mine[z, slot] + got[z, c].astype(F32)

                @pl.when(zl == z)
                def _():
                    mine[z, slot] = total

                @pl.when(zl != z)
                def _():
                    zsend[slot] = total.astype(BF16)
                    send(zsend.at[slot], zgot.at[slot], z_send.at[slot], z_recv.at[slot], hd=at_z)
            return 0

        lax.fori_loop(0, steps, step, 0)

    def weights_across():
        await_recv(wo_a.at[half, :], w_recv.at[0])
        await_recv(wo_b.at[half, :], w_recv.at[1])
        send(wo_a.at[half, :], wo_a.at[half, :], wc_send.at[0], wc_recv.at[0], ctx=sibling)
        send(wo_b.at[half, :], wo_b.at[half, :], wc_send.at[1], wc_recv.at[1], ctx=sibling)

    def weights_end():
        await_recv(wo_a.at[other_half, :], wc_recv.at[0])
        await_recv(wo_b.at[other_half, :], wc_recv.at[1])

    for q in range(4):
        pass_on(q, me, 0, zmate)
    acc[...] = jnp.zeros_like(acc)
    peak[...] = jnp.full(peak.shape, -1e30, F32)
    gather_own(0)
    gather_mate(0)
    gather_own(1)
    gather_mate(1)
    gather_near(0)
    gather_own(2)
    gather_mate(2)
    gather_far(0)
    gather_end(0)

    plan = ((0, 0), (1, 0), (2, 0), (3, 0), (1, 1), (2, 1), (3, 1), (2, 2), (3, 2), (3, 3))
    after = {
        0: lambda: (gather_near(1), weights_across()),
        1: lambda: (gather_own(3), gather_mate(3), gather_far(1)),
        2: lambda: gather_near(2),
        3: lambda: (gather_end(1), weights_end()),
        4: lambda: (finish(0), finish(1), exchange(0), gather_far(2), gather_near(3)),
        6: lambda: (gather_end(2), project_far(0)),
        7: lambda: (finish(2), gather_far(3), project_near(0)),
        8: lambda: (gather_end(3), sum_up(0)),
    }

    def attention_step(i, _):
        g, q = jnp.int32(0), jnp.int32(0)
        for k, (gk, qk) in enumerate(plan):
            g, q = jnp.where(i == k, gk, g), jnp.where(i == k, qk, q)

        @pl.when(g == q)
        def _():
            attend(g, q, True)

        @pl.when(g != q)
        def _():
            attend(g, q, False)

        for k, work in after.items():
            pl.when(i == k)(lambda work=work: (work(), None)[1])
        return 0

    lax.fori_loop(0, len(plan), attention_step, 0)
    finish(3)
    exchange(1)
    project_far(1)
    project_near(1)
    sum_up(1)

    own_rows = zl

    def final_step(slot, _):
        await_recv(zgot.at[slot], z_recv.at[slot])
        cols = pl.ds(pl.multiple_of(slot * width, width), width)
        out_ref[:, cols] = (mine[own_rows, slot] + zgot[slot].astype(F32)).astype(BF16)
        return 0

    lax.fori_loop(0, 2 * steps, final_step, 0)

    for copy in sends:
        copy.wait_send()

    def await_send(src, ssem):
        pltpu.make_async_remote_copy(
            src_ref=src, dst_ref=src, send_sem=ssem, recv_sem=ssem,
            device_id=(me, head), device_id_type=MESH,
        ).wait_send()

    for i in range(1, N_CTX):
        target = (me + i) % N_CTX
        await_send(stage.at[target], a2a_send.at[target])

    def drain_kv(q, _):
        for way in range(4):
            await_send(kv.at[q, me], kv_send.at[q, me, way])
        for way in range(1, 4):
            await_send(kv.at[q, zmate], kv_send.at[q, zmate, way])
        for dz in range(2):
            for dx in range(1, 4):
                src = ctx_at(dz, dx, 0)
                await_send(kv.at[q, src], kv_send.at[q, src, 3])
        await_send(kv.at[q, ctx_at(0, 3, 0)], kv_send.at[q, ctx_at(0, 3, 0), 1])
        await_send(kv.at[q, ctx_at(1, 1, 0)], kv_send.at[q, ctx_at(1, 1, 0), 2])
        return 0

    lax.fori_loop(0, 4, drain_kv, 0)
    await_send(wo_a.at[half, :], wc_send.at[0])
    await_send(wo_b.at[half, :], wc_send.at[1])

    def drain(c, _):
        for z in range(2):
            await_send(part_a.at[z, c], part_send.at[z, 0, c])
            await_send(part_b.at[z, c], part_send.at[z, 1, c])
            await_send(att.at[0, 0], att_send.at[z, c])
        await_send(zsend.at[c], z_send.at[c])
        await_send(zsend.at[steps + c], z_send.at[steps + c])
        return 0

    lax.fori_loop(0, steps, drain, 0)


def body(hidden_states, norm_gain, query_weight, key_weight, value_weight, output_weight, keep_flags, span_order):
    base, inner = rope_tables()
    vmem = pl.BlockSpec(memory_space=pltpu.VMEM)
    smem = pl.BlockSpec(memory_space=pltpu.SMEM)
    anywhere = pl.BlockSpec(memory_space=pl.ANY)
    dma = pltpu.SemaphoreType.DMA
    return pl.pallas_call(
        kernel,
        out_shape=jax.ShapeDtypeStruct((64, 4096), BF16),
        in_specs=[anywhere, vmem, anywhere, anywhere, anywhere, anywhere, smem, smem, anywhere, vmem],
        out_specs=vmem,
        scratch_shapes=[
            pltpu.VMEM((32, 32, 4096), BF16),
            pltpu.VMEM((4096, 768), BF16),
            pltpu.VMEM((512, 4096), BF16),
            pltpu.VMEM((512, 2048), BF16),
            pltpu.VMEM((512, 2048), BF16),
            pltpu.VMEM((32, 2, 1, 128), F32),
            pltpu.VMEM((256, 4096), BF16),
            pltpu.VMEM((1, 128), jnp.int32),
            pltpu.VMEM((16, 1, 128), jnp.int32),
            pltpu.SMEM((16, 1, 128), jnp.int32),
            pltpu.VMEM((16, 2, 6, 32, 128), BF16),
            pltpu.VMEM((16, 2, 6, 32, 128), BF16),
            pltpu.VMEM((2048, 128), BF16),
            pltpu.VMEM((4, 16, 2, 128, 128), BF16),
            pltpu.VMEM((2048, 256), F32),
            pltpu.VMEM((2048, 128), F32),
            pltpu.VMEM((4, 2, 64, 512), BF16),
            pltpu.VMEM((2, 2, 64, 512), BF16),
            pltpu.VMEM((2, 2, 64, 512), BF16),
            pltpu.VMEM((2, 4, 64, 512), BF16),
            pltpu.VMEM((2, 4, 64, 512), BF16),
            pltpu.VMEM((2, 4, 64, 512), BF16),
            pltpu.VMEM((2, 4, 64, 512), BF16),
            pltpu.VMEM((2, 8, 64, 512), F32),
            pltpu.VMEM((8, 64, 512), BF16),
            pltpu.VMEM((8, 64, 512), BF16),
            dma((8,)),
            dma((16,)), dma((16,)),
            dma((16,)), dma((16,)),
            dma((4, 16, 4)), dma((4, 16)),
            dma((2,)), dma((2,)), dma((2,)), dma((2,)),
            dma((2, 4)), dma((2, 4)),
            dma((2, 2, 4)), dma((2, 2, 4)),
            dma((8,)), dma((8,)),
            dma,
        ],
        compiler_params=pltpu.CompilerParams(
            collective_id=1, has_side_effects=True, vmem_limit_bytes=60 * 2**20
        ),
        name="prefill",
    )(
        hidden_states.reshape(32, 32, 4096), norm_gain.reshape(1, 4096), query_weight, key_weight, value_weight, output_weight,
        keep_flags, span_order, jnp.asarray(base), jnp.asarray(inner),
    )


def solution(mesh):
    return jax.shard_map(
        body,
        mesh=mesh,
        in_specs=(
            P("ctx", None),
            P(),
            P(None, "head"),
            P(None, "head"),
            P(None, "head"),
            P("head", None),
            P("ctx"),
            P(),
        ),
        out_specs=P(("ctx", "head"), None),
        check_vma=False,
    )
```

```python
import functools
import math

import jax
import jax.numpy as jnp
import numpy as np
from jax import lax
from jax.experimental import pallas as pl
from jax.experimental.pallas import tpu as pltpu
from jax.sharding import PartitionSpec as P

MESH = pl.DeviceIdType.MESH
HEAD_DIM = 128
PIECE = 32
KEPT = 16
SPAN = 512
N_CTX = 16
LOG2E = math.log2(math.e)
F32 = jnp.float32
BF16 = jnp.bfloat16


def rope_tables():
    frequency = 500000.0 ** (-2.0 * np.arange(64, dtype=np.float64) / HEAD_DIM)
    frequency = np.concatenate([frequency, frequency])[None, :]
    sign = np.concatenate([-np.ones(64), np.ones(64)])[None, :]
    pieces = np.arange(N_CTX * 2 * SPAN // PIECE, dtype=np.float64)[:, None] * PIECE * frequency
    rows = np.arange(PIECE, dtype=np.float64)[:, None] * frequency
    base = np.stack([np.cos(pieces), np.sin(pieces)]).reshape(2, N_CTX, 32, 1, HEAD_DIM)
    inner = np.stack([np.cos(rows), np.sin(rows), np.cos(rows) * sign, np.sin(rows) * sign])
    return base.transpose(1, 2, 0, 3, 4).astype(np.float32), inner.astype(np.float32)


def kernel(
    hidden_hbm, gain_ref, wq_hbm, wk_hbm, wv_hbm, wo_hbm, flags_ref, order_ref, base_hbm, inner_ref,
    out_ref,
    hidden, wq, wkv, wo, wo_a, wo_b, base, normed, flag_src, flag_all, flag_sm,
    kv_raw, q_raw, kv_stage, q_stage, kv_got, q_got,
    queries, kv, acc, peak, att, att_a, att_b, part_a, part_b, got_a, got_b, mine, zsend, zgot,
    hidden_sem, load_sem, flag_send, flag_recv, kva_send, kva_recv, qa_send, qa_recv, kv_send, kv_recv, w_send, w_recv, wc_send, wc_recv,
    att_send, att_recv, part_send, part_recv, z_send, z_recv, local_sem,
):
    me = lax.axis_index("ctx")
    head = lax.axis_index("head")
    zh, x, core = me // 8, (me // 2) % 4, me % 2
    zl, y = head // 4, head % 4
    pa = y + 1 - 2 * (y % 2)
    pb = 3 - y

    def ctx_at(dz, dx, dc):
        return ((zh + dz) % 2) * 8 + ((x + dx) % 4) * 2 + (core + dc) % 2

    def send(src, dst, ssem, rsem, ctx=None, hd=None):
        copy = pltpu.make_async_remote_copy(
            src_ref=src, dst_ref=dst, send_sem=ssem, recv_sem=rsem,
            device_id=(me if ctx is None else ctx, head if hd is None else hd),
            device_id_type=MESH,
        )
        copy.start()
        return copy

    def await_recv(dst, rsem):
        pltpu.make_async_remote_copy(
            src_ref=dst, dst_ref=dst, send_sem=rsem, recv_sem=rsem,
            device_id=(me, head), device_id_type=MESH,
        ).wait_recv()

    sends = []

    def hidden_part(c):
        part = pl.ds(c * 8, 8)
        return pltpu.make_async_copy(hidden_hbm.at[part], hidden.at[part], hidden_sem.at[c])

    loads = []

    def load(src, dst):
        copy = pltpu.make_async_copy(src, dst, load_sem.at[len(loads)])
        copy.start()
        loads.append(copy)
        return copy

    hidden_part(0).start()
    load_k = load(wk_hbm, wkv.at[:, pl.ds(0, 128)])
    load_v = load(wv_hbm, wkv.at[:, pl.ds(128, 128)])
    load_base = load(base_hbm.at[me], base)
    for c in range(1, 4):
        hidden_part(c).start()
    load_q = load(wq_hbm, wq)
    load_o = load(wo_hbm, wo)

    barrier = pltpu.get_barrier_semaphore()
    for i in range(1, N_CTX):
        pl.semaphore_signal(barrier, inc=1, device_id=((me + i) % N_CTX, head), device_id_type=MESH)
    for hd in (zl * 4 + pa, zl * 4 + pb, (1 - zl) * 4 + y):
        pl.semaphore_signal(barrier, inc=1, device_id=(me, hd), device_id_type=MESH)
    pl.semaphore_wait(barrier, N_CTX - 1 + 3)

    lane = lax.broadcasted_iota(jnp.int32, (1, 128), 1)
    own_flags = jnp.where(lane == 0, flags_ref[0], jnp.where(lane == 1, flags_ref[1], 0))
    flag_src[...] = own_flags
    flag_all[me] = own_flags
    for i in range(1, N_CTX):
        sends.append(send(flag_src, flag_all.at[me], flag_send.at[i], flag_recv.at[me], ctx=(me + i) % N_CTX))

    load_base.wait()
    load_k.wait()
    load_v.wait()

    def rope_of(piece):
        cos_base, sin_base = base[piece, 0], base[piece, 1]
        return (
            cos_base * inner_ref[0] - sin_base * inner_ref[1],
            sin_base * inner_ref[2] + cos_base * inner_ref[3],
        )

    def turned(block, rope):
        return (block * rope[0] + pltpu.roll(block, 64, 1) * rope[1]).astype(BF16)

    def norm_piece(piece, _):
        total = jnp.zeros((PIECE, 128), F32)
        for c in range(0, 4096, 512):
            part = hidden[piece, :, c:c + 512].astype(F32)
            part = part * part
            total += (part[:, :128] + part[:, 128:256]) + (part[:, 256:384] + part[:, 384:])
        scale = lax.rsqrt(jnp.sum(total, axis=1, keepdims=True) * (1.0 / 4096) + 1e-05)
        for c in range(0, 4096, 512):
            part = hidden[piece, :, c:c + 512].astype(F32)
            normed[piece, :, c:c + 512] = (part * scale * gain_ref[:, c:c + 512]).astype(BF16)
        return 0

    def project_kv(c, _):
        hidden_part(c).wait()
        lax.fori_loop(c * 8, c * 8 + 8, norm_piece, 0)
        rows = normed[pl.ds(c * 8, 8)].reshape(256, 4096)
        projected = jnp.dot(rows, wkv[...], preferred_element_type=F32)
        for i in range(8):
            block = projected[i * PIECE:(i + 1) * PIECE]
            kv_raw[c * 8 + i, 0] = turned(block[:, :128], rope_of(c * 8 + i))
            kv_raw[c * 8 + i, 1] = block[:, 128:].astype(BF16)
        return 0

    lax.fori_loop(0, 4, project_kv, 0)

    load_o.wait()
    half = pl.ds(core * 256, 256)
    other_half = pl.ds((1 - core) * 256, 256)
    cols_a, cols_b = pl.ds(0, 2048), pl.ds(2048, 2048)
    sends.append(send(wo.at[half, cols_a], wo_a.at[half, :], w_send.at[0], w_recv.at[0], hd=zl * 4 + pa))
    sends.append(send(wo.at[half, cols_b], wo_b.at[half, :], w_send.at[1], w_recv.at[1], hd=zl * 4 + pb))

    for i in range(1, N_CTX):
        src = (me + i) % N_CTX
        await_recv(flag_all.at[src], flag_recv.at[src])
    to_scalars = pltpu.make_async_copy(flag_all, flag_sm, local_sem)
    to_scalars.start()
    to_scalars.wait()

    first_rank = jnp.int32(0)
    for i in range(N_CTX):
        first_rank += jnp.where(i < me, flag_sm[i, 0, 0] + flag_sm[i, 0, 1], 0)

    def shift_of(rank):
        return order_ref[rank] % N_CTX

    slot_span = (1 - flag_sm[me, 0, 0], jnp.int32(1))
    slot_shift = (shift_of(jnp.minimum(first_rank, KEPT - 1)), shift_of(jnp.minimum(first_rank + 1, KEPT - 1)))

    routes = (
        (1, 2, 0), (1, 2, 1), (0, 1, 0), (0, 3, 1), (1, 1, 0), (1, 3, 1), (0, 2, 0), (0, 2, 1),
        (1, 1, 1), (1, 3, 0), (0, 1, 1), (0, 3, 0), (1, 0, 0), (1, 0, 1), (0, 0, 1),
    )

    def spread(raw, stage, got, ssem, rsem):
        for route in routes + ((0, 0, 0),):
            target = ctx_at(*route)
            for slot in range(2):
                piece = slot_span[slot] * 16 + (target + N_CTX - slot_shift[slot]) % N_CTX
                stage[target, slot] = raw[piece]
            if route != (0, 0, 0):
                send(stage.at[target], got.at[me], ssem.at[target], rsem.at[me], ctx=target)
            else:
                got[me] = stage[target]

    def collect(got, rsem):
        for route in routes:
            src = ctx_at(*route)
            await_recv(got.at[src], rsem.at[src])

    spread(kv_raw, kv_stage, kv_got, kva_send, kva_recv)

    load_q.wait()

    def project_q(c, _):
        rows = normed[pl.ds(c * 8, 8)].reshape(256, 4096)
        projected = jnp.dot(rows, wq[...], preferred_element_type=F32)
        for i in range(8):
            rope = rope_of(c * 8 + i)
            for part in range(4):
                block = projected[i * PIECE:(i + 1) * PIECE, part * 128:(part + 1) * 128]
                q_raw[c * 8 + i, part] = turned(block, rope)
        return 0

    lax.fori_loop(0, 4, project_q, 0)
    spread(q_raw, q_stage, q_got, qa_send, qa_recv)

    arrival = [jnp.int32(0)] * KEPT
    rank = jnp.int32(0)
    for i in range(N_CTX):
        f0, f1 = flag_sm[i, 0, 0], flag_sm[i, 0, 1]
        for flag, place in ((f0, 2 * i), (f1, 2 * i + f0)):
            for r in range(KEPT):
                arrival[r] = jnp.where((flag == 1) & (rank == r), place, arrival[r])
            rank = rank + flag
    arrival = [(place // 2, place % 2) for place in arrival]

    collect(kv_got, kva_recv)
    for r in range(KEPT):
        src, slot = arrival[r]
        rows = slice((r % 4) * 32, (r % 4) * 32 + 32)
        kv[r // 4, me, 0, rows, :] = kv_got[src, slot, 0]
        kv[r // 4, me, 1, rows, :] = kv_got[src, slot, 1]

    sibling = ctx_at(0, 0, 1)
    zmate = ctx_at(1, 0, 0)
    xplus, xminus = ctx_at(0, 1, 0), ctx_at(0, 3, 0)

    def pass_on(q, src, way, target):
        send(kv.at[q, src], kv.at[q, src], kv_send.at[q, src, way], kv_recv.at[q, src], ctx=target)

    def arrived(q, src):
        await_recv(kv.at[q, src], kv_recv.at[q, src])

    def gather_own(q):
        pass_on(q, me, 1, xplus)
        pass_on(q, me, 2, xminus)
        pass_on(q, me, 3, sibling)

    def gather_mate(q):
        arrived(q, zmate)
        pass_on(q, zmate, 1, xplus)
        pass_on(q, zmate, 2, xminus)
        pass_on(q, zmate, 3, sibling)

    def gather_near(q):
        for dz in range(2):
            left, right = ctx_at(dz, 3, 0), ctx_at(dz, 1, 0)
            arrived(q, left)
            if dz == 0:
                pass_on(q, left, 1, xplus)
            pass_on(q, left, 3, sibling)
            arrived(q, right)
            if dz == 1:
                pass_on(q, right, 2, xminus)
            pass_on(q, right, 3, sibling)

    def gather_far(q):
        for dz in range(2):
            across = ctx_at(dz, 2, 0)
            arrived(q, across)
            pass_on(q, across, 3, sibling)

    def gather_end(q):
        for dz in range(2):
            for dx in range(4):
                arrived(q, ctx_at(dz, dx, 1))

    factor = LOG2E / math.sqrt(HEAD_DIM)
    block_rows = 128
    blocks = 512 // block_rows

    def attend(g, q, masked):
        keys = kv[q, :, 0].reshape(2048, 128)
        values = jnp.concatenate([kv[q, :, 1].reshape(2048, 128), jnp.ones((2048, 128), BF16)], axis=1)
        if masked:
            key_lane = lax.broadcasted_iota(jnp.int32, (1, 2048), 1)
            key_pos = jnp.zeros((1, 2048), jnp.int32)
            for b in range(4):
                place = (key_lane // 128 + N_CTX - shift_of(4 * q + b)) % N_CTX
                here = (key_lane % 128) // 32 == b
                key_pos = jnp.where(here, b * SPAN + place * PIECE + key_lane % PIECE, key_pos)

        def rows_of(a):
            return pl.ds(pl.multiple_of(g * 512 + a * block_rows, block_rows), block_rows)

        def score(a):
            return lax.dot_general(
                queries[rows_of(a), :], keys, (((1,), (1,)), ((), ())), preferred_element_type=F32
            )

        scores = score(0)
        for a in range(blocks):
            rows = rows_of(a)
            coming = score(a + 1) if a + 1 < blocks else None
            if masked:
                row = lax.broadcasted_iota(jnp.int32, (block_rows, 1), 0) % PIECE
                query_pos = a * SPAN + ((me + N_CTX - shift_of(4 * q + a)) % N_CTX) * PIECE + row
                scores = jnp.where(key_pos <= query_pos, scores, -1e30)
            old = peak[rows, :]
            new = jnp.maximum(old, jnp.max(scores, axis=1, keepdims=True))
            peak[rows, :] = new
            expo = jnp.exp2((scores - new[:, :1]) * factor).astype(BF16)
            fade = jnp.exp2((old - new) * factor)
            mixed = jnp.dot(expo, values, preferred_element_type=F32)
            acc[rows, :] = acc[rows, :] * jnp.concatenate([fade, fade], axis=1) + mixed
            scores = coming

    def finish(g):
        for r in range(4 * g, 4 * g + 4):
            hd = r // 2
            for part in range(4):
                rows = slice(r * 128 + part * 32, r * 128 + part * 32 + 32)
                value = (acc[rows, :128] / acc[rows, 128:]).astype(BF16)
                att[hd % 4, hd // 4, (r % 2) * 32:(r % 2) * 32 + 32, part * 128:(part + 1) * 128] = value

    far = (y + 2) % 4
    at_pa, at_pb, at_z = zl * 4 + pa, zl * 4 + pb, (1 - zl) * 4 + y
    att_moves = ((far, att_a, 1, at_pa), (far, att_b, 1, at_pb), (pa, att_a, 0, at_pa), (pb, att_b, 0, at_pb))

    def exchange(z):
        for i, (block, dst, slot, hd) in enumerate(att_moves):
            send(att.at[block, z], dst.at[slot, z], att_send.at[z, i], att_recv.at[z, i], hd=hd)

    def term(rows, weights):
        return jnp.dot(rows, weights, preferred_element_type=F32).astype(BF16).astype(F32)

    width = 512
    steps = 2048 // width

    def two_cols(c):
        return (
            pl.ds(pl.multiple_of(c * width, width), width),
            pl.ds(pl.multiple_of(2048 + c * width, width), width),
        )

    def project_out(z):
        for i in range(4):
            await_recv(att_a.at[0, z], att_recv.at[z, i])

        def step(c, _):
            cols, cols_b = two_cols(c)
            sides = (
                (0, cols, pb, att_a, wo_a, part_a, got_a, at_pb),
                (1, cols_b, pa, att_b, wo_b, part_b, got_b, at_pa),
            )
            for side, own_cols, other, att_s, wo_s, part_s, got_s, hd in sides:
                own = jnp.concatenate([att[other, z], att[y, z]], axis=0)
                theirs = jnp.concatenate([att_s[1, z], att_s[0, z]], axis=0)
                total = term(own, wo[:, own_cols]) + term(theirs, wo_s[:, cols])
                part_s[z, c] = total[:64].astype(BF16)
                send(part_s.at[z, c], got_s.at[z, c], part_send.at[z, side, c], part_recv.at[z, side, c], hd=hd)
                mine[z, side * steps + c] = total[64:]
            return 0

        lax.fori_loop(0, steps, step, 0)

    def sum_up(z):
        def step(c, _):
            for side, got in ((0, got_a), (1, got_b)):
                slot = side * steps + c
                await_recv(got.at[z, c], part_recv.at[z, side, c])
                total = mine[z, slot] + got[z, c].astype(F32)

                @pl.when(zl == z)
                def _():
                    mine[z, slot] = total

                @pl.when(zl != z)
                def _():
                    zsend[slot] = total.astype(BF16)
                    send(zsend.at[slot], zgot.at[slot], z_send.at[slot], z_recv.at[slot], hd=at_z)
            return 0

        lax.fori_loop(0, steps, step, 0)

    def weights_across():
        await_recv(wo_a.at[half, :], w_recv.at[0])
        await_recv(wo_b.at[half, :], w_recv.at[1])
        send(wo_a.at[half, :], wo_a.at[half, :], wc_send.at[0], wc_recv.at[0], ctx=sibling)
        send(wo_b.at[half, :], wo_b.at[half, :], wc_send.at[1], wc_recv.at[1], ctx=sibling)

    def weights_end():
        await_recv(wo_a.at[other_half, :], wc_recv.at[0])
        await_recv(wo_b.at[other_half, :], wc_recv.at[1])

    for q in range(4):
        pass_on(q, me, 0, zmate)
    gather_own(0)
    gather_own(1)
    acc[...] = jnp.zeros_like(acc)
    peak[...] = jnp.full(peak.shape, -1e30, F32)
    gather_mate(0)
    gather_mate(1)
    gather_near(0)
    gather_own(2)
    gather_mate(2)
    collect(q_got, qa_recv)
    for r in range(KEPT):
        src, slot = arrival[r]
        queries[r * 128:(r + 1) * 128, :] = q_got[src, slot].reshape(128, 128)
    gather_far(0)
    gather_end(0)

    plan = ((0, 0), (1, 0), (2, 0), (3, 0), (1, 1), (2, 1), (3, 1), (2, 2), (3, 2), (3, 3))
    after = {
        0: lambda: (gather_near(1), weights_across()),
        1: lambda: (gather_own(3), gather_mate(3), gather_far(1)),
        2: lambda: gather_near(2),
        3: lambda: (gather_end(1), weights_end()),
        4: lambda: (finish(0), finish(1), exchange(0), gather_far(2), gather_near(3)),
        6: lambda: (gather_end(2), project_out(0)),
        7: lambda: (finish(2), gather_far(3)),
        8: lambda: (gather_end(3), sum_up(0)),
    }

    def attention_step(i, _):
        g, q = jnp.int32(0), jnp.int32(0)
        for k, (gk, qk) in enumerate(plan):
            g, q = jnp.where(i == k, gk, g), jnp.where(i == k, qk, q)

        @pl.when(g == q)
        def _():
            attend(g, q, True)

        @pl.when(g != q)
        def _():
            attend(g, q, False)

        for k, work in after.items():
            pl.when(i == k)(lambda work=work: (work(), None)[1])
        return 0

    lax.fori_loop(0, len(plan), attention_step, 0)
    finish(3)
    exchange(1)
    project_out(1)
    sum_up(1)

    own_rows = zl

    def final_step(slot, _):
        await_recv(zgot.at[slot], z_recv.at[slot])
        cols = pl.ds(pl.multiple_of(slot * width, width), width)
        out_ref[:, cols] = (mine[own_rows, slot] + zgot[slot].astype(F32)).astype(BF16)
        return 0

    lax.fori_loop(0, 2 * steps, final_step, 0)

    for copy in sends:
        copy.wait_send()

    def await_send(src, ssem):
        pltpu.make_async_remote_copy(
            src_ref=src, dst_ref=src, send_sem=ssem, recv_sem=ssem,
            device_id=(me, head), device_id_type=MESH,
        ).wait_send()

    for i in range(1, N_CTX):
        target = (me + i) % N_CTX
        await_send(kv_stage.at[target], kva_send.at[target])
        await_send(q_stage.at[target], qa_send.at[target])

    def drain_kv(q, _):
        for way in range(4):
            await_send(kv.at[q, me], kv_send.at[q, me, way])
        for way in range(1, 4):
            await_send(kv.at[q, zmate], kv_send.at[q, zmate, way])
        for dz in range(2):
            for dx in range(1, 4):
                src = ctx_at(dz, dx, 0)
                await_send(kv.at[q, src], kv_send.at[q, src, 3])
        await_send(kv.at[q, ctx_at(0, 3, 0)], kv_send.at[q, ctx_at(0, 3, 0), 1])
        await_send(kv.at[q, ctx_at(1, 1, 0)], kv_send.at[q, ctx_at(1, 1, 0), 2])
        return 0

    lax.fori_loop(0, 4, drain_kv, 0)
    await_send(wo_a.at[half, :], wc_send.at[0])
    await_send(wo_b.at[half, :], wc_send.at[1])

    def drain(c, _):
        for z in range(2):
            await_send(part_a.at[z, c], part_send.at[z, 0, c])
            await_send(part_b.at[z, c], part_send.at[z, 1, c])
            await_send(att.at[0, 0], att_send.at[z, c])
        await_send(zsend.at[c], z_send.at[c])
        await_send(zsend.at[steps + c], z_send.at[steps + c])
        return 0

    lax.fori_loop(0, steps, drain, 0)


def body(hidden_states, norm_gain, query_weight, key_weight, value_weight, output_weight, keep_flags, span_order):
    base, inner = rope_tables()
    vmem = pl.BlockSpec(memory_space=pltpu.VMEM)
    smem = pl.BlockSpec(memory_space=pltpu.SMEM)
    anywhere = pl.BlockSpec(memory_space=pl.ANY)
    dma = pltpu.SemaphoreType.DMA
    return pl.pallas_call(
        kernel,
        out_shape=jax.ShapeDtypeStruct((64, 4096), BF16),
        in_specs=[anywhere, vmem, anywhere, anywhere, anywhere, anywhere, smem, smem, anywhere, vmem],
        out_specs=vmem,
        scratch_shapes=[
            pltpu.VMEM((32, 32, 4096), BF16),
            pltpu.VMEM((4096, 512), BF16),
            pltpu.VMEM((4096, 256), BF16),
            pltpu.VMEM((512, 4096), BF16),
            pltpu.VMEM((512, 2048), BF16),
            pltpu.VMEM((512, 2048), BF16),
            pltpu.VMEM((32, 2, 1, 128), F32),
            pltpu.VMEM((32, 32, 4096), BF16),
            pltpu.VMEM((1, 128), jnp.int32),
            pltpu.VMEM((16, 1, 128), jnp.int32),
            pltpu.SMEM((16, 1, 128), jnp.int32),
            pltpu.VMEM((32, 2, 32, 128), BF16),
            pltpu.VMEM((32, 4, 32, 128), BF16),
            pltpu.VMEM((16, 2, 2, 32, 128), BF16),
            pltpu.VMEM((16, 2, 4, 32, 128), BF16),
            pltpu.VMEM((16, 2, 2, 32, 128), BF16),
            pltpu.VMEM((16, 2, 4, 32, 128), BF16),
            pltpu.VMEM((2048, 128), BF16),
            pltpu.VMEM((4, 16, 2, 128, 128), BF16),
            pltpu.VMEM((2048, 256), F32),
            pltpu.VMEM((2048, 128), F32),
            pltpu.VMEM((4, 2, 64, 512), BF16),
            pltpu.VMEM((2, 2, 64, 512), BF16),
            pltpu.VMEM((2, 2, 64, 512), BF16),
            pltpu.VMEM((2, 4, 64, 512), BF16),
            pltpu.VMEM((2, 4, 64, 512), BF16),
            pltpu.VMEM((2, 4, 64, 512), BF16),
            pltpu.VMEM((2, 4, 64, 512), BF16),
            pltpu.VMEM((2, 8, 64, 512), F32),
            pltpu.VMEM((8, 64, 512), BF16),
            pltpu.VMEM((8, 64, 512), BF16),
            dma((4,)),
            dma((8,)),
            dma((16,)), dma((16,)),
            dma((16,)), dma((16,)),
            dma((16,)), dma((16,)),
            dma((4, 16, 4)), dma((4, 16)),
            dma((2,)), dma((2,)), dma((2,)), dma((2,)),
            dma((2, 4)), dma((2, 4)),
            dma((2, 2, 4)), dma((2, 2, 4)),
            dma((8,)), dma((8,)),
            dma,
        ],
        compiler_params=pltpu.CompilerParams(
            collective_id=1, has_side_effects=True, vmem_limit_bytes=60 * 2**20
        ),
        name="prefill",
    )(
        hidden_states.reshape(32, 32, 4096), norm_gain.reshape(1, 4096), query_weight, key_weight, value_weight, output_weight,
        keep_flags, span_order, jnp.asarray(base), jnp.asarray(inner),
    )


def solution(mesh):
    return jax.shard_map(
        body,
        mesh=mesh,
        in_specs=(
            P("ctx", None),
            P(),
            P(None, "head"),
            P(None, "head"),
            P(None, "head"),
            P("head", None),
            P("ctx"),
            P(),
        ),
        out_specs=P(("ctx", "head"), None),
        check_vma=False,
    )
```

```python
import functools
import math

import jax
import jax.numpy as jnp
import numpy as np
from jax import lax
from jax.experimental import pallas as pl
from jax.experimental.pallas import tpu as pltpu
from jax.sharding import PartitionSpec as P

MESH = pl.DeviceIdType.MESH
HEAD_DIM = 128
PIECE = 32
KEPT = 16
SPAN = 512
N_CTX = 16
LOG2E = math.log2(math.e)
F32 = jnp.float32
BF16 = jnp.bfloat16


def rope_tables():
    frequency = 500000.0 ** (-2.0 * np.arange(64, dtype=np.float64) / HEAD_DIM)
    frequency = np.concatenate([frequency, frequency])[None, :]
    sign = np.concatenate([-np.ones(64), np.ones(64)])[None, :]
    pieces = np.arange(N_CTX * 2 * SPAN // PIECE, dtype=np.float64)[:, None] * PIECE * frequency
    rows = np.arange(PIECE, dtype=np.float64)[:, None] * frequency
    base = np.stack([np.cos(pieces), np.sin(pieces)]).reshape(2, N_CTX, 32, 1, HEAD_DIM)
    inner = np.stack([np.cos(rows), np.sin(rows), np.cos(rows) * sign, np.sin(rows) * sign])
    return base.transpose(1, 2, 0, 3, 4).astype(np.float32), inner.astype(np.float32)


def kernel(
    hidden_hbm, gain_ref, wq_hbm, wk_hbm, wv_hbm, wo_hbm, flags_ref, order_ref, base_hbm, inner_ref,
    out_ref,
    hidden, wq, wkv, wo, wo_a, wo_b, base, normed, flag_src, flag_all, flag_sm,
    kv_raw, q_raw, kv_stage, q_stage, kv_got, q_got,
    queries, kv, acc, peak, att, att_a, att_b, part_a, part_b, got_a, got_b, mine, zsend, zgot,
    hidden_sem, load_sem, flag_send, flag_recv, kva_send, kva_recv, qa_send, qa_recv, kv_send, kv_recv, w_send, w_recv, wc_send, wc_recv,
    att_send, att_recv, part_send, part_recv, z_send, z_recv, local_sem,
):
    me = lax.axis_index("ctx")
    head = lax.axis_index("head")
    zh, x, core = me // 8, (me // 2) % 4, me % 2
    zl, y = head // 4, head % 4
    pa = y + 1 - 2 * (y % 2)
    pb = 3 - y

    def ctx_at(dz, dx, dc):
        return ((zh + dz) % 2) * 8 + ((x + dx) % 4) * 2 + (core + dc) % 2

    def send(src, dst, ssem, rsem, ctx=None, hd=None):
        copy = pltpu.make_async_remote_copy(
            src_ref=src, dst_ref=dst, send_sem=ssem, recv_sem=rsem,
            device_id=(me if ctx is None else ctx, head if hd is None else hd),
            device_id_type=MESH,
        )
        copy.start()
        return copy

    def await_recv(dst, rsem):
        pltpu.make_async_remote_copy(
            src_ref=dst, dst_ref=dst, send_sem=rsem, recv_sem=rsem,
            device_id=(me, head), device_id_type=MESH,
        ).wait_recv()

    sends = []

    def hidden_part(c):
        part = pl.ds(c * 8, 8)
        return pltpu.make_async_copy(hidden_hbm.at[part], hidden.at[part], hidden_sem.at[c])

    loads = []

    def load(src, dst):
        copy = pltpu.make_async_copy(src, dst, load_sem.at[len(loads)])
        copy.start()
        loads.append(copy)
        return copy

    hidden_part(0).start()
    load_k = load(wk_hbm, wkv.at[:, pl.ds(0, 128)])
    load_v = load(wv_hbm, wkv.at[:, pl.ds(128, 128)])
    load_base = load(base_hbm.at[me], base)
    for c in range(1, 4):
        hidden_part(c).start()
    load_q = load(wq_hbm, wq)
    load_o = load(wo_hbm, wo)

    barrier = pltpu.get_barrier_semaphore()
    for i in range(1, N_CTX):
        pl.semaphore_signal(barrier, inc=1, device_id=((me + i) % N_CTX, head), device_id_type=MESH)
    for hd in (zl * 4 + pa, zl * 4 + pb, (1 - zl) * 4 + y):
        pl.semaphore_signal(barrier, inc=1, device_id=(me, hd), device_id_type=MESH)

    load_base.wait()
    load_k.wait()
    load_v.wait()

    def rope_of(piece):
        cos_base, sin_base = base[piece, 0], base[piece, 1]
        return (
            cos_base * inner_ref[0] - sin_base * inner_ref[1],
            sin_base * inner_ref[2] + cos_base * inner_ref[3],
        )

    def turned(block, rope):
        return (block * rope[0] + pltpu.roll(block, 64, 1) * rope[1]).astype(BF16)

    def norm_piece(piece, _):
        total = jnp.zeros((PIECE, 128), F32)
        for c in range(0, 4096, 512):
            part = hidden[piece, :, c:c + 512].astype(F32)
            part = part * part
            total += (part[:, :128] + part[:, 128:256]) + (part[:, 256:384] + part[:, 384:])
        scale = lax.rsqrt(jnp.sum(total, axis=1, keepdims=True) * (1.0 / 4096) + 1e-05)
        for c in range(0, 4096, 512):
            part = hidden[piece, :, c:c + 512].astype(F32)
            normed[piece, :, c:c + 512] = (part * scale * gain_ref[:, c:c + 512]).astype(BF16)
        return 0

    def project_kv(c, _):
        hidden_part(c).wait()
        lax.fori_loop(c * 8, c * 8 + 8, norm_piece, 0)
        rows = normed[pl.ds(c * 8, 8)].reshape(256, 4096)
        projected = jnp.dot(rows, wkv[...], preferred_element_type=F32)
        for i in range(8):
            block = projected[i * PIECE:(i + 1) * PIECE]
            kv_raw[c * 8 + i, 0] = turned(block[:, :128], rope_of(c * 8 + i))
            kv_raw[c * 8 + i, 1] = block[:, 128:].astype(BF16)
        return 0

    lax.fori_loop(0, 1, project_kv, 0)

    pl.semaphore_wait(barrier, N_CTX - 1 + 3)

    lane = lax.broadcasted_iota(jnp.int32, (1, 128), 1)
    own_flags = jnp.where(lane == 0, flags_ref[0], jnp.where(lane == 1, flags_ref[1], 0))
    flag_src[...] = own_flags
    flag_all[me] = own_flags
    for i in range(1, N_CTX):
        sends.append(send(flag_src, flag_all.at[me], flag_send.at[i], flag_recv.at[me], ctx=(me + i) % N_CTX))

    lax.fori_loop(1, 4, project_kv, 0)

    load_o.wait()
    half = pl.ds(core * 256, 256)
    other_half = pl.ds((1 - core) * 256, 256)
    cols_a, cols_b = pl.ds(0, 2048), pl.ds(2048, 2048)
    sends.append(send(wo.at[half, cols_a], wo_a.at[half, :], w_send.at[0], w_recv.at[0], hd=zl * 4 + pa))
    sends.append(send(wo.at[half, cols_b], wo_b.at[half, :], w_send.at[1], w_recv.at[1], hd=zl * 4 + pb))

    for i in range(1, N_CTX):
        src = (me + i) % N_CTX
        await_recv(flag_all.at[src], flag_recv.at[src])
    to_scalars = pltpu.make_async_copy(flag_all, flag_sm, local_sem)
    to_scalars.start()
    to_scalars.wait()

    first_rank = jnp.int32(0)
    for i in range(N_CTX):
        first_rank += jnp.where(i < me, flag_sm[i, 0, 0] + flag_sm[i, 0, 1], 0)

    def shift_of(rank):
        return order_ref[rank] % N_CTX

    slot_span = (1 - flag_sm[me, 0, 0], jnp.int32(1))
    slot_shift = (shift_of(jnp.minimum(first_rank, KEPT - 1)), shift_of(jnp.minimum(first_rank + 1, KEPT - 1)))

    routes = (
        (1, 2, 0), (1, 2, 1), (0, 1, 0), (0, 3, 1), (1, 1, 0), (1, 3, 1), (0, 2, 0), (0, 2, 1),
        (1, 1, 1), (1, 3, 0), (0, 1, 1), (0, 3, 0), (1, 0, 0), (1, 0, 1), (0, 0, 1),
    )

    def arrange(raw, stage, route):
        target = ctx_at(*route)
        for slot in range(2):
            piece = slot_span[slot] * 16 + (target + N_CTX - slot_shift[slot]) % N_CTX
            stage[target, slot] = raw[piece]

    def part_with(stage, got, ssem, rsem, route):
        target = ctx_at(*route)
        send(stage.at[target], got.at[me], ssem.at[target], rsem.at[me], ctx=target)

    def collect(got, rsem):
        for route in routes:
            src = ctx_at(*route)
            await_recv(got.at[src], rsem.at[src])

    for route in routes:
        arrange(kv_raw, kv_stage, route)
        part_with(kv_stage, kv_got, kva_send, kva_recv, route)
    arrange(kv_raw, kv_stage, (0, 0, 0))
    kv_got[me] = kv_stage[me]

    load_q.wait()

    def project_q(c, _):
        rows = normed[pl.ds(c * 8, 8)].reshape(256, 4096)
        projected = jnp.dot(rows, wq[...], preferred_element_type=F32)
        for i in range(8):
            rope = rope_of(c * 8 + i)
            for part in range(4):
                block = projected[i * PIECE:(i + 1) * PIECE, part * 128:(part + 1) * 128]
                q_raw[c * 8 + i, part] = turned(block, rope)
        return 0

    lax.fori_loop(0, 4, project_q, 0)
    for route in routes + ((0, 0, 0),):
        arrange(q_raw, q_stage, route)
    q_got[me] = q_stage[me]

    arrival = [jnp.int32(0)] * KEPT
    rank = jnp.int32(0)
    for i in range(N_CTX):
        f0, f1 = flag_sm[i, 0, 0], flag_sm[i, 0, 1]
        for flag, place in ((f0, 2 * i), (f1, 2 * i + f0)):
            for r in range(KEPT):
                arrival[r] = jnp.where((flag == 1) & (rank == r), place, arrival[r])
            rank = rank + flag
    arrival = [(place // 2, place % 2) for place in arrival]

    def place_of(dz, dx, dc):
        return ((x + dx) % 4) * 4 + ((zh + dz) % 2) * 2 + (core + dc) % 2

    own_place = place_of(0, 0, 0)
    collect(kv_got, kva_recv)
    for r in range(KEPT):
        src, slot = arrival[r]
        rows = slice((r % 4) * 32, (r % 4) * 32 + 32)
        kv[r // 4, own_place, 0, rows, :] = kv_got[src, slot, 0]
        kv[r // 4, own_place, 1, rows, :] = kv_got[src, slot, 1]

    sibling = ctx_at(0, 0, 1)
    zmate = ctx_at(1, 0, 0)
    xplus, xminus = ctx_at(0, 1, 0), ctx_at(0, 3, 0)

    def pass_on(q, src, way, target):
        place = place_of(*src)
        send(kv.at[q, place], kv.at[q, place], kv_send.at[q, place, way], kv_recv.at[q, place], ctx=target)

    def arrived(q, src):
        place = place_of(*src)
        await_recv(kv.at[q, place], kv_recv.at[q, place])

    def gather_own(q):
        pass_on(q, (0, 0, 0), 1, xplus)
        pass_on(q, (0, 0, 0), 2, xminus)
        pass_on(q, (0, 0, 0), 3, sibling)

    def gather_mate(q):
        arrived(q, (1, 0, 0))
        pass_on(q, (1, 0, 0), 1, xplus)
        pass_on(q, (1, 0, 0), 2, xminus)
        pass_on(q, (1, 0, 0), 3, sibling)

    def gather_near(q):
        for dz in range(2):
            arrived(q, (dz, 3, 0))
            if dz == 0:
                pass_on(q, (dz, 3, 0), 1, xplus)
            pass_on(q, (dz, 3, 0), 3, sibling)
            arrived(q, (dz, 1, 0))
            if dz == 1:
                pass_on(q, (dz, 1, 0), 2, xminus)
            pass_on(q, (dz, 1, 0), 3, sibling)

    def gather_far(q):
        for dz in range(2):
            arrived(q, (dz, 2, 0))
            pass_on(q, (dz, 2, 0), 3, sibling)

    def gather_end(q, dx):
        for dz in range(2):
            arrived(q, (dz, dx, 1))

    factor = LOG2E / math.sqrt(HEAD_DIM)
    block_rows = 128

    def attend(g, at_x):
        sources = pl.ds(pl.multiple_of(at_x * 4, 4), 4)

        def rows_of(a):
            return slice((4 * g + a) * block_rows, (4 * g + a + 1) * block_rows)

        def keys_or_values(a, which):
            seen = 32 * (a + 1)
            last = kv[g, sources, which, :seen].reshape(4 * seen, 128)
            if g == 0:
                return last
            return jnp.concatenate([kv[:g, sources, which].reshape(g * 512, 128), last], axis=0)

        def score(a):
            return lax.dot_general(
                queries[rows_of(a), :], keys_or_values(a, 0), (((1,), (1,)), ((), ())), preferred_element_type=F32
            )

        def visible(a):
            seen = 32 * (a + 1)
            lane = lax.broadcasted_iota(jnp.int32, (1, 4 * seen), 1)
            source, within = lane // seen, lane % seen
            owner = (source // 2) * 8 + at_x * 2 + source % 2
            shift = shift_of(4 * g + a)
            key_pos = ((owner + N_CTX - shift) % N_CTX) * PIECE + within - a * PIECE
            key_pos = jnp.where(within < a * PIECE, -1, key_pos)
            row = lax.broadcasted_iota(jnp.int32, (block_rows, 1), 0) % PIECE
            return key_pos <= ((me + N_CTX - shift) % N_CTX) * PIECE + row

        scores = score(0)
        for a in range(4):
            rows = rows_of(a)
            coming = score(a + 1) if a < 3 else None
            last = jnp.where(visible(a), scores[:, g * 512:], -1e30)
            scores = last if g == 0 else jnp.concatenate([scores[:, :g * 512], last], axis=1)
            old = peak[rows, :]
            new = jnp.maximum(old, jnp.max(scores, axis=1, keepdims=True))
            peak[rows, :] = new
            expo = jnp.exp2((scores - new[:, :1]) * factor).astype(BF16)
            fade = jnp.exp2((old - new) * factor)
            values = keys_or_values(a, 1)
            values = jnp.concatenate([values, jnp.ones(values.shape, BF16)], axis=1)
            mixed = jnp.dot(expo, values, preferred_element_type=F32)
            acc[rows, :] = acc[rows, :] * jnp.concatenate([fade, fade], axis=1) + mixed
            scores = coming

    def finish(g):
        for r in range(4 * g, 4 * g + 4):
            hd = r // 2
            for part in range(4):
                rows = slice(r * 128 + part * 32, r * 128 + part * 32 + 32)
                value = (acc[rows, :128] / acc[rows, 128:]).astype(BF16)
                att[hd % 4, hd // 4, (r % 2) * 32:(r % 2) * 32 + 32, part * 128:(part + 1) * 128] = value

    far = (y + 2) % 4
    at_pa, at_pb, at_z = zl * 4 + pa, zl * 4 + pb, (1 - zl) * 4 + y
    att_moves = ((far, att_a, 1, at_pa), (far, att_b, 1, at_pb), (pa, att_a, 0, at_pa), (pb, att_b, 0, at_pb))

    def exchange(z):
        for i, (block, dst, slot, hd) in enumerate(att_moves):
            send(att.at[block, z], dst.at[slot, z], att_send.at[z, i], att_recv.at[z, i], hd=hd)

    def term(rows, weights):
        return jnp.dot(rows, weights, preferred_element_type=F32).astype(BF16).astype(F32)

    width = 512
    steps = 2048 // width

    def two_cols(c):
        return (
            pl.ds(pl.multiple_of(c * width, width), width),
            pl.ds(pl.multiple_of(2048 + c * width, width), width),
        )

    def exchanged(z):
        for i in range(4):
            await_recv(att_a.at[0, z], att_recv.at[z, i])

    def project_out(z, first, last):
        def step(c, _):
            cols, cols_b = two_cols(c)
            sides = (
                (0, cols, pb, att_a, wo_a, part_a, got_a, at_pb),
                (1, cols_b, pa, att_b, wo_b, part_b, got_b, at_pa),
            )
            for side, own_cols, other, att_s, wo_s, part_s, got_s, hd in sides:
                own = jnp.concatenate([att[other, z], att[y, z]], axis=0)
                theirs = jnp.concatenate([att_s[1, z], att_s[0, z]], axis=0)
                total = term(own, wo[:, own_cols]) + term(theirs, wo_s[:, cols])
                part_s[z, c] = total[:64].astype(BF16)
                send(part_s.at[z, c], got_s.at[z, c], part_send.at[z, side, c], part_recv.at[z, side, c], hd=hd)
                mine[z, side * steps + c] = total[64:]
            return 0

        lax.fori_loop(first, last, step, 0)

    def sum_up(z, first, last):
        def step(c, _):
            for side, got in ((0, got_a), (1, got_b)):
                slot = side * steps + c
                await_recv(got.at[z, c], part_recv.at[z, side, c])
                total = mine[z, slot] + got[z, c].astype(F32)

                @pl.when(zl == z)
                def _():
                    mine[z, slot] = total

                @pl.when(zl != z)
                def _():
                    zsend[slot] = total.astype(BF16)
                    send(zsend.at[slot], zgot.at[slot], z_send.at[slot], z_recv.at[slot], hd=at_z)
            return 0

        lax.fori_loop(first, last, step, 0)

    def weights_across():
        await_recv(wo_a.at[half, :], w_recv.at[0])
        await_recv(wo_b.at[half, :], w_recv.at[1])
        send(wo_a.at[half, :], wo_a.at[half, :], wc_send.at[0], wc_recv.at[0], ctx=sibling)
        send(wo_b.at[half, :], wo_b.at[half, :], wc_send.at[1], wc_recv.at[1], ctx=sibling)

    def weights_end():
        await_recv(wo_a.at[other_half, :], wc_recv.at[0])
        await_recv(wo_b.at[other_half, :], wc_recv.at[1])

    for q in range(4):
        pass_on(q, (0, 0, 0), 0, zmate)
    for route in routes[:8]:
        part_with(q_stage, q_got, qa_send, qa_recv, route)
    gather_own(0)
    gather_own(1)
    gather_own(2)
    gather_own(3)
    for route in routes[8:]:
        part_with(q_stage, q_got, qa_send, qa_recv, route)
    acc[...] = jnp.zeros_like(acc)
    peak[...] = jnp.full(peak.shape, -1e30, F32)
    for q in range(4):
        gather_mate(q)
    collect(q_got, qa_recv)
    for r in range(KEPT):
        src, slot = arrival[r]
        queries[r * 128:(r + 1) * 128, :] = q_got[src, slot].reshape(128, 128)
    for q in range(4):
        gather_end(q, 0)

    before = {(i, g): (lambda i=i, g=g: gather_end(g, (0, 1, 3, 2)[i])) for i in range(1, 4) for g in range(4)}
    after = {(0, g): (lambda g=g: gather_near(g)) for g in range(4)}
    after.update({(2, g): (lambda g=g: gather_far(g)) for g in range(4)})
    after[1, 1] = weights_across
    after[2, 3] = lambda: (gather_far(3), weights_end())
    after[3, 1] = lambda: (finish(0), finish(1), exchange(0))
    after[3, 2] = lambda: finish(2)

    def attention_pass(i, _):
        at_x = (x + jnp.where(i == 3, 2, jnp.where(i == 2, 3, i))) % 4
        for g in range(4):
            for k in range(4):
                if (k, g) in before:
                    pl.when(i == k)(lambda work=before[k, g]: (work(), None)[1])
            attend(g, at_x)
            for k in range(4):
                if (k, g) in after:
                    pl.when(i == k)(lambda work=after[k, g]: (work(), None)[1])
        return 0

    lax.fori_loop(0, 4, attention_pass, 0)
    finish(3)
    exchange(1)
    turns = ((0, 0, 2), (1, 0, 1), (0, 2, 3), (1, 1, 2), (0, 3, 4), (1, 2, 4))
    exchanged(0)
    for k, turn in enumerate(turns):
        if k == 1:
            exchanged(1)
        project_out(*turn)
    for turn in turns:
        sum_up(*turn)

    own_rows = zl

    def final_step(slot, _):
        await_recv(zgot.at[slot], z_recv.at[slot])
        cols = pl.ds(pl.multiple_of(slot * width, width), width)
        out_ref[:, cols] = (mine[own_rows, slot] + zgot[slot].astype(F32)).astype(BF16)
        return 0

    lax.fori_loop(0, 2 * steps, final_step, 0)

    for copy in sends:
        copy.wait_send()

    def await_send(src, ssem):
        pltpu.make_async_remote_copy(
            src_ref=src, dst_ref=src, send_sem=ssem, recv_sem=ssem,
            device_id=(me, head), device_id_type=MESH,
        ).wait_send()

    for i in range(1, N_CTX):
        target = (me + i) % N_CTX
        await_send(kv_stage.at[target], kva_send.at[target])
        await_send(q_stage.at[target], qa_send.at[target])

    def drain_kv(q, _):
        def sent(src, way):
            place = place_of(*src)
            await_send(kv.at[q, place], kv_send.at[q, place, way])

        for way in range(4):
            sent((0, 0, 0), way)
        for way in range(1, 4):
            sent((1, 0, 0), way)
        for dz in range(2):
            for dx in range(1, 4):
                sent((dz, dx, 0), 3)
        sent((0, 3, 0), 1)
        sent((1, 1, 0), 2)
        return 0

    lax.fori_loop(0, 4, drain_kv, 0)
    await_send(wo_a.at[half, :], wc_send.at[0])
    await_send(wo_b.at[half, :], wc_send.at[1])

    def drain(c, _):
        for z in range(2):
            await_send(part_a.at[z, c], part_send.at[z, 0, c])
            await_send(part_b.at[z, c], part_send.at[z, 1, c])
            await_send(att.at[0, 0], att_send.at[z, c])
        await_send(zsend.at[c], z_send.at[c])
        await_send(zsend.at[steps + c], z_send.at[steps + c])
        return 0

    lax.fori_loop(0, steps, drain, 0)


def body(hidden_states, norm_gain, query_weight, key_weight, value_weight, output_weight, keep_flags, span_order):
    base, inner = rope_tables()
    vmem = pl.BlockSpec(memory_space=pltpu.VMEM)
    smem = pl.BlockSpec(memory_space=pltpu.SMEM)
    anywhere = pl.BlockSpec(memory_space=pl.ANY)
    dma = pltpu.SemaphoreType.DMA
    return pl.pallas_call(
        kernel,
        out_shape=jax.ShapeDtypeStruct((64, 4096), BF16),
        in_specs=[anywhere, vmem, anywhere, anywhere, anywhere, anywhere, smem, smem, anywhere, vmem],
        out_specs=vmem,
        scratch_shapes=[
            pltpu.VMEM((32, 32, 4096), BF16),
            pltpu.VMEM((4096, 512), BF16),
            pltpu.VMEM((4096, 256), BF16),
            pltpu.VMEM((512, 4096), BF16),
            pltpu.VMEM((512, 2048), BF16),
            pltpu.VMEM((512, 2048), BF16),
            pltpu.VMEM((32, 2, 1, 128), F32),
            pltpu.VMEM((32, 32, 4096), BF16),
            pltpu.VMEM((1, 128), jnp.int32),
            pltpu.VMEM((16, 1, 128), jnp.int32),
            pltpu.SMEM((16, 1, 128), jnp.int32),
            pltpu.VMEM((32, 2, 32, 128), BF16),
            pltpu.VMEM((32, 4, 32, 128), BF16),
            pltpu.VMEM((16, 2, 2, 32, 128), BF16),
            pltpu.VMEM((16, 2, 4, 32, 128), BF16),
            pltpu.VMEM((16, 2, 2, 32, 128), BF16),
            pltpu.VMEM((16, 2, 4, 32, 128), BF16),
            pltpu.VMEM((2048, 128), BF16),
            pltpu.VMEM((4, 16, 2, 128, 128), BF16),
            pltpu.VMEM((2048, 256), F32),
            pltpu.VMEM((2048, 128), F32),
            pltpu.VMEM((4, 2, 64, 512), BF16),
            pltpu.VMEM((2, 2, 64, 512), BF16),
            pltpu.VMEM((2, 2, 64, 512), BF16),
            pltpu.VMEM((2, 4, 64, 512), BF16),
            pltpu.VMEM((2, 4, 64, 512), BF16),
            pltpu.VMEM((2, 4, 64, 512), BF16),
            pltpu.VMEM((2, 4, 64, 512), BF16),
            pltpu.VMEM((2, 8, 64, 512), F32),
            pltpu.VMEM((8, 64, 512), BF16),
            pltpu.VMEM((8, 64, 512), BF16),
            dma((4,)),
            dma((8,)),
            dma((16,)), dma((16,)),
            dma((16,)), dma((16,)),
            dma((16,)), dma((16,)),
            dma((4, 16, 4)), dma((4, 16)),
            dma((2,)), dma((2,)), dma((2,)), dma((2,)),
            dma((2, 4)), dma((2, 4)),
            dma((2, 2, 4)), dma((2, 2, 4)),
            dma((8,)), dma((8,)),
            dma,
        ],
        compiler_params=pltpu.CompilerParams(
            collective_id=1, has_side_effects=True, vmem_limit_bytes=60 * 2**20
        ),
        name="prefill",
    )(
        hidden_states.reshape(32, 32, 4096), norm_gain.reshape(1, 4096), query_weight, key_weight, value_weight, output_weight,
        keep_flags, span_order, jnp.asarray(base), jnp.asarray(inner),
    )


def solution(mesh):
    return jax.shard_map(
        body,
        mesh=mesh,
        in_specs=(
            P("ctx", None),
            P(),
            P(None, "head"),
            P(None, "head"),
            P(None, "head"),
            P("head", None),
            P("ctx"),
            P(),
        ),
        out_specs=P(("ctx", "head"), None),
        check_vma=False,
    )
```

```python
import functools
import math

import jax
import jax.numpy as jnp
import numpy as np
from jax import lax
from jax.experimental import pallas as pl
from jax.experimental.pallas import tpu as pltpu
from jax.sharding import PartitionSpec as P

MESH = pl.DeviceIdType.MESH
HEAD_DIM = 128
PIECE = 32
KEPT = 16
SPAN = 512
N_CTX = 16
LOG2E = math.log2(math.e)
F32 = jnp.float32
BF16 = jnp.bfloat16


def rope_tables():
    frequency = 500000.0 ** (-2.0 * np.arange(64, dtype=np.float64) / HEAD_DIM)
    frequency = np.concatenate([frequency, frequency])[None, :]
    sign = np.concatenate([-np.ones(64), np.ones(64)])[None, :]
    pieces = np.arange(N_CTX * 2 * SPAN // PIECE, dtype=np.float64)[:, None] * PIECE * frequency
    rows = np.arange(PIECE, dtype=np.float64)[:, None] * frequency
    base = np.stack([np.cos(pieces), np.sin(pieces)]).reshape(2, N_CTX, 32, 1, HEAD_DIM)
    inner = np.stack([np.cos(rows), np.sin(rows), np.cos(rows) * sign, np.sin(rows) * sign])
    return base.transpose(1, 2, 0, 3, 4).astype(np.float32), inner.astype(np.float32)


def kernel(
    hidden_hbm, gain_ref, wq_hbm, wk_hbm, wv_hbm, wo_hbm, flags_ref, order_ref, base_hbm, inner_ref,
    out_ref,
    hidden, wq, wkv, wo, wo_a, wo_b, base, normed, flag_src, flag_all, flag_sm,
    kv_raw, q_raw, kv_stage, q_stage, kv_got, q_got,
    queries, kv, acc, peak, att, att_a, att_b, part_a, part_b, got_a, got_b, mine, zsend, zgot,
    hidden_sem, load_sem, flag_send, flag_recv, kva_send, kva_recv, qa_send, qa_recv, kv_send, kv_recv, w_send, w_recv, wc_send, wc_recv,
    att_send, att_recv, part_send, part_recv, z_send, z_recv, local_sem,
):
    me = lax.axis_index("ctx")
    head = lax.axis_index("head")
    zh, x, core = me // 8, (me // 2) % 4, me % 2
    zl, y = head // 4, head % 4
    pa = y + 1 - 2 * (y % 2)
    pb = 3 - y

    def ctx_at(dz, dx, dc):
        return ((zh + dz) % 2) * 8 + ((x + dx) % 4) * 2 + (core + dc) % 2

    def send(src, dst, ssem, rsem, ctx=None, hd=None):
        copy = pltpu.make_async_remote_copy(
            src_ref=src, dst_ref=dst, send_sem=ssem, recv_sem=rsem,
            device_id=(me if ctx is None else ctx, head if hd is None else hd),
            device_id_type=MESH,
        )
        copy.start()
        return copy

    def await_recv(dst, rsem):
        pltpu.make_async_remote_copy(
            src_ref=dst, dst_ref=dst, send_sem=rsem, recv_sem=rsem,
            device_id=(me, head), device_id_type=MESH,
        ).wait_recv()

    sends = []

    def hidden_part(c):
        part = pl.ds(c * 8, 8)
        return pltpu.make_async_copy(hidden_hbm.at[part], hidden.at[part], hidden_sem.at[c])

    loads = []

    def load(src, dst):
        copy = pltpu.make_async_copy(src, dst, load_sem.at[len(loads)])
        copy.start()
        loads.append(copy)
        return copy

    hidden_part(0).start()
    load_k = load(wk_hbm, wkv.at[:, pl.ds(0, 128)])
    load_v = load(wv_hbm, wkv.at[:, pl.ds(128, 128)])
    load_base = load(base_hbm.at[me], base)
    for c in range(1, 4):
        hidden_part(c).start()
    load_q = load(wq_hbm, wq)
    load_o = load(wo_hbm, wo)

    barrier = pltpu.get_barrier_semaphore()
    for i in range(1, N_CTX):
        pl.semaphore_signal(barrier, inc=1, device_id=((me + i) % N_CTX, head), device_id_type=MESH)
    for hd in (zl * 4 + pa, zl * 4 + pb, (1 - zl) * 4 + y):
        pl.semaphore_signal(barrier, inc=1, device_id=(me, hd), device_id_type=MESH)

    load_base.wait()
    load_k.wait()
    load_v.wait()

    def rope_of(piece):
        cos_base, sin_base = base[piece, 0], base[piece, 1]
        return (
            cos_base * inner_ref[0] - sin_base * inner_ref[1],
            sin_base * inner_ref[2] + cos_base * inner_ref[3],
        )

    def turned(block, rope):
        return (block * rope[0] + pltpu.roll(block, 64, 1) * rope[1]).astype(BF16)

    def norm_piece(piece, _):
        total = jnp.zeros((PIECE, 128), F32)
        for c in range(0, 4096, 512):
            part = hidden[piece, :, c:c + 512].astype(F32)
            part = part * part
            total += (part[:, :128] + part[:, 128:256]) + (part[:, 256:384] + part[:, 384:])
        scale = lax.rsqrt(jnp.sum(total, axis=1, keepdims=True) * (1.0 / 4096) + 1e-05)
        for c in range(0, 4096, 512):
            part = hidden[piece, :, c:c + 512].astype(F32)
            normed[piece, :, c:c + 512] = (part * scale * gain_ref[:, c:c + 512]).astype(BF16)
        return 0

    def project_kv(c, _):
        hidden_part(c).wait()
        lax.fori_loop(c * 8, c * 8 + 8, norm_piece, 0)
        rows = normed[pl.ds(c * 8, 8)].reshape(256, 4096)
        projected = jnp.dot(rows, wkv[...], preferred_element_type=F32)
        for i in range(8):
            block = projected[i * PIECE:(i + 1) * PIECE]
            kv_raw[c * 8 + i, 0] = turned(block[:, :128], rope_of(c * 8 + i))
            kv_raw[c * 8 + i, 1] = block[:, 128:].astype(BF16)
        return 0

    lax.fori_loop(0, 1, project_kv, 0)

    pl.semaphore_wait(barrier, N_CTX - 1 + 3)

    lane = lax.broadcasted_iota(jnp.int32, (1, 128), 1)
    own_flags = jnp.where(lane == 0, flags_ref[0], jnp.where(lane == 1, flags_ref[1], 0))
    flag_src[...] = own_flags
    flag_all[me] = own_flags
    for i in range(1, N_CTX):
        sends.append(send(flag_src, flag_all.at[me], flag_send.at[i], flag_recv.at[me], ctx=(me + i) % N_CTX))

    lax.fori_loop(1, 4, project_kv, 0)

    load_o.wait()
    half = pl.ds(core * 256, 256)
    other_half = pl.ds((1 - core) * 256, 256)
    cols_a, cols_b = pl.ds(0, 2048), pl.ds(2048, 2048)
    sends.append(send(wo.at[half, cols_a], wo_a.at[half, :], w_send.at[0], w_recv.at[0], hd=zl * 4 + pa))
    sends.append(send(wo.at[half, cols_b], wo_b.at[half, :], w_send.at[1], w_recv.at[1], hd=zl * 4 + pb))

    for i in range(1, N_CTX):
        src = (me + i) % N_CTX
        await_recv(flag_all.at[src], flag_recv.at[src])
    to_scalars = pltpu.make_async_copy(flag_all, flag_sm, local_sem)
    to_scalars.start()
    to_scalars.wait()

    first_rank = jnp.int32(0)
    for i in range(N_CTX):
        first_rank += jnp.where(i < me, flag_sm[i, 0, 0] + flag_sm[i, 0, 1], 0)

    def shift_of(rank):
        return order_ref[rank] % N_CTX

    slot_span = (1 - flag_sm[me, 0, 0], jnp.int32(1))
    slot_shift = (shift_of(jnp.minimum(first_rank, KEPT - 1)), shift_of(jnp.minimum(first_rank + 1, KEPT - 1)))

    routes = (
        (1, 2, 0), (1, 2, 1), (0, 1, 0), (0, 3, 1), (1, 1, 0), (1, 3, 1), (0, 2, 0), (0, 2, 1),
        (1, 1, 1), (1, 3, 0), (0, 1, 1), (0, 3, 0), (1, 0, 0), (1, 0, 1), (0, 0, 1),
    )

    def arrange(raw, stage, route):
        target = ctx_at(*route)
        for slot in range(2):
            piece = slot_span[slot] * 16 + (target + N_CTX - slot_shift[slot]) % N_CTX
            stage[target, slot] = raw[piece]

    def part_with(stage, got, ssem, rsem, route):
        target = ctx_at(*route)
        send(stage.at[target], got.at[me], ssem.at[target], rsem.at[me], ctx=target)

    def collect(got, rsem):
        for route in routes:
            src = ctx_at(*route)
            await_recv(got.at[src], rsem.at[src])

    for route in routes:
        arrange(kv_raw, kv_stage, route)
        part_with(kv_stage, kv_got, kva_send, kva_recv, route)
    arrange(kv_raw, kv_stage, (0, 0, 0))
    kv_got[me] = kv_stage[me]

    load_q.wait()

    def project_q(c, _):
        rows = normed[pl.ds(c * 8, 8)].reshape(256, 4096)
        projected = jnp.dot(rows, wq[...], preferred_element_type=F32)
        for i in range(8):
            rope = rope_of(c * 8 + i)
            for part in range(4):
                block = projected[i * PIECE:(i + 1) * PIECE, part * 128:(part + 1) * 128]
                q_raw[c * 8 + i, part] = turned(block, rope)
        return 0

    lax.fori_loop(0, 4, project_q, 0)
    for route in routes + ((0, 0, 0),):
        arrange(q_raw, q_stage, route)
    q_got[me] = q_stage[me]

    arrival = [jnp.int32(0)] * KEPT
    rank = jnp.int32(0)
    for i in range(N_CTX):
        f0, f1 = flag_sm[i, 0, 0], flag_sm[i, 0, 1]
        for flag, place in ((f0, 2 * i), (f1, 2 * i + f0)):
            for r in range(KEPT):
                arrival[r] = jnp.where((flag == 1) & (rank == r), place, arrival[r])
            rank = rank + flag
    arrival = [(place // 2, place % 2) for place in arrival]

    def place_of(dz, dx, dc):
        return ((x + dx) % 4) * 4 + ((zh + dz) % 2) * 2 + (core + dc) % 2

    own_place = place_of(0, 0, 0)
    collect(kv_got, kva_recv)
    for r in range(KEPT):
        src, slot = arrival[r]
        rows = slice((r % 4) * 32, (r % 4) * 32 + 32)
        kv[r // 4, own_place, 0, rows, :] = kv_got[src, slot, 0]
        kv[r // 4, own_place, 1, rows, :] = kv_got[src, slot, 1]

    sibling = ctx_at(0, 0, 1)
    zmate = ctx_at(1, 0, 0)
    xplus, xminus = ctx_at(0, 1, 0), ctx_at(0, 3, 0)

    def pass_on(q, src, way, target):
        place = place_of(*src)
        send(kv.at[q, place], kv.at[q, place], kv_send.at[q, place, way], kv_recv.at[q, place], ctx=target)

    def arrived(q, src):
        place = place_of(*src)
        await_recv(kv.at[q, place], kv_recv.at[q, place])

    def gather_own(q):
        pass_on(q, (0, 0, 0), 1, xplus)
        pass_on(q, (0, 0, 0), 2, xminus)
        pass_on(q, (0, 0, 0), 3, sibling)

    def gather_mate(q):
        arrived(q, (1, 0, 0))
        pass_on(q, (1, 0, 0), 1, xplus)
        pass_on(q, (1, 0, 0), 2, xminus)
        pass_on(q, (1, 0, 0), 3, sibling)

    def gather_near(q):
        for dz in range(2):
            arrived(q, (dz, 3, 0))
            if dz == 0:
                pass_on(q, (dz, 3, 0), 1, xplus)
            pass_on(q, (dz, 3, 0), 3, sibling)
            arrived(q, (dz, 1, 0))
            if dz == 1:
                pass_on(q, (dz, 1, 0), 2, xminus)
            pass_on(q, (dz, 1, 0), 3, sibling)

    def gather_far(q):
        for dz in range(2):
            arrived(q, (dz, 2, 0))
            pass_on(q, (dz, 2, 0), 3, sibling)

    def gather_end(q, dx):
        for dz in range(2):
            arrived(q, (dz, dx, 1))

    factor = LOG2E / math.sqrt(HEAD_DIM)
    block_rows = 128

    def attend(g, at_x):
        sources = pl.ds(pl.multiple_of(at_x * 4, 4), 4)

        def rows_of(a):
            return slice((4 * g + a) * block_rows, (4 * g + a + 1) * block_rows)

        def keys_or_values(a, which):
            seen = 32 * (a + 1)
            last = kv[g, sources, which, :seen].reshape(4 * seen, 128)
            if g == 0:
                return last
            return jnp.concatenate([kv[:g, sources, which].reshape(g * 512, 128), last], axis=0)

        def score(a):
            return lax.dot_general(
                queries[rows_of(a), :], keys_or_values(a, 0), (((1,), (1,)), ((), ())), preferred_element_type=F32
            )

        def visible(a):
            seen = 32 * (a + 1)
            lane = lax.broadcasted_iota(jnp.int32, (1, 4 * seen), 1)
            source, within = lane // seen, lane % seen
            owner = (source // 2) * 8 + at_x * 2 + source % 2
            shift = shift_of(4 * g + a)
            key_pos = ((owner + N_CTX - shift) % N_CTX) * PIECE + within - a * PIECE
            key_pos = jnp.where(within < a * PIECE, -1, key_pos)
            row = lax.broadcasted_iota(jnp.int32, (block_rows, 1), 0) % PIECE
            return key_pos <= ((me + N_CTX - shift) % N_CTX) * PIECE + row

        scores = score(0)
        for a in range(4):
            rows = rows_of(a)
            coming = score(a + 1) if a < 3 else None
            last = jnp.where(visible(a), scores[:, g * 512:], -1e30)
            scores = last if g == 0 else jnp.concatenate([scores[:, :g * 512], last], axis=1)
            old = peak[rows, :]
            new = jnp.maximum(old, jnp.max(scores, axis=1, keepdims=True))
            peak[rows, :] = new
            expo = jnp.exp2((scores - new[:, :1]) * factor).astype(BF16)
            fade = jnp.exp2((old - new) * factor)
            values = keys_or_values(a, 1)
            values = jnp.concatenate([values, jnp.ones(values.shape, BF16)], axis=1)
            mixed = jnp.dot(expo, values, preferred_element_type=F32)
            acc[rows, :] = acc[rows, :] * jnp.concatenate([fade, fade], axis=1) + mixed
            scores = coming

    def finish(g):
        for r in range(4 * g, 4 * g + 4):
            hd = r // 2
            for part in range(4):
                rows = slice(r * 128 + part * 32, r * 128 + part * 32 + 32)
                value = (acc[rows, :128] / acc[rows, 128:]).astype(BF16)
                att[hd % 4, hd // 4, (r % 2) * 32:(r % 2) * 32 + 32, part * 128:(part + 1) * 128] = value

    far = (y + 2) % 4
    at_pa, at_pb, at_z = zl * 4 + pa, zl * 4 + pb, (1 - zl) * 4 + y
    att_moves = ((far, att_a, 1, at_pa), (far, att_b, 1, at_pb), (pa, att_a, 0, at_pa), (pb, att_b, 0, at_pb))

    def exchange(z):
        for i, (block, dst, slot, hd) in enumerate(att_moves):
            send(att.at[block, z], dst.at[slot, z], att_send.at[z, i], att_recv.at[z, i], hd=hd)

    def term(rows, weights):
        return jnp.dot(rows, weights, preferred_element_type=F32).astype(BF16).astype(F32)

    width = 512
    steps = 2048 // width

    def two_cols(c):
        return (
            pl.ds(pl.multiple_of(c * width, width), width),
            pl.ds(pl.multiple_of(2048 + c * width, width), width),
        )

    def exchanged(z):
        for i in range(4):
            await_recv(att_a.at[0, z], att_recv.at[z, i])

    def project_out(z, first, last):
        def step(c, _):
            cols, cols_b = two_cols(c)
            sides = (
                (0, cols, pb, att_a, wo_a, part_a, got_a, at_pb),
                (1, cols_b, pa, att_b, wo_b, part_b, got_b, at_pa),
            )
            for side, own_cols, other, att_s, wo_s, part_s, got_s, hd in sides:
                own = jnp.concatenate([att[other, z], att[y, z]], axis=0)
                theirs = jnp.concatenate([att_s[1, z], att_s[0, z]], axis=0)
                total = term(own, wo[:, own_cols]) + term(theirs, wo_s[:, cols])
                part_s[z, c] = total[:64].astype(BF16)
                send(part_s.at[z, c], got_s.at[z, c], part_send.at[z, side, c], part_recv.at[z, side, c], hd=hd)
                mine[z, side * steps + c] = total[64:]
            return 0

        lax.fori_loop(first, last, step, 0)

    def sum_up(z, first, last):
        def step(c, _):
            for side, got in ((0, got_a), (1, got_b)):
                slot = side * steps + c
                await_recv(got.at[z, c], part_recv.at[z, side, c])
                total = mine[z, slot] + got[z, c].astype(F32)

                @pl.when(zl == z)
                def _():
                    mine[z, slot] = total

                @pl.when(zl != z)
                def _():
                    zsend[slot] = total.astype(BF16)
                    send(zsend.at[slot], zgot.at[slot], z_send.at[slot], z_recv.at[slot], hd=at_z)
            return 0

        lax.fori_loop(first, last, step, 0)

    def weights_across():
        await_recv(wo_a.at[half, :], w_recv.at[0])
        await_recv(wo_b.at[half, :], w_recv.at[1])
        send(wo_a.at[half, :], wo_a.at[half, :], wc_send.at[0], wc_recv.at[0], ctx=sibling)
        send(wo_b.at[half, :], wo_b.at[half, :], wc_send.at[1], wc_recv.at[1], ctx=sibling)

    def weights_end():
        await_recv(wo_a.at[other_half, :], wc_recv.at[0])
        await_recv(wo_b.at[other_half, :], wc_recv.at[1])

    for q in range(4):
        pass_on(q, (0, 0, 0), 0, zmate)
    for route in routes[:8]:
        part_with(q_stage, q_got, qa_send, qa_recv, route)
    gather_own(0)
    gather_own(1)
    gather_own(2)
    gather_own(3)
    for route in routes[8:]:
        part_with(q_stage, q_got, qa_send, qa_recv, route)
    acc[...] = jnp.zeros_like(acc)
    peak[...] = jnp.full(peak.shape, -1e30, F32)
    for q in range(4):
        gather_mate(q)
    collect(q_got, qa_recv)
    for r in range(KEPT):
        src, slot = arrival[r]
        queries[r * 128:(r + 1) * 128, :] = q_got[src, slot].reshape(128, 128)
    for q in range(4):
        gather_end(q, 0)

    before = {(i, g): (lambda i=i, g=g: gather_end(g, (0, 1, 3, 2)[i])) for i in range(1, 4) for g in range(4)}
    after = {
        (0, 1): lambda: gather_near(0),
        (0, 2): lambda: gather_near(1),
        (0, 3): lambda: (gather_near(2), gather_near(3)),
    }
    after.update({(2, g): (lambda g=g: gather_far(g)) for g in range(4)})
    after[1, 1] = weights_across
    after[2, 3] = lambda: (gather_far(3), weights_end())
    after[3, 1] = lambda: (finish(0), finish(1), exchange(0))
    after[3, 2] = lambda: finish(2)

    def attention_pass(i, _):
        at_x = (x + jnp.where(i == 3, 2, jnp.where(i == 2, 3, i))) % 4
        for g in range(4):
            for k in range(4):
                if (k, g) in before:
                    pl.when(i == k)(lambda work=before[k, g]: (work(), None)[1])
            attend(g, at_x)
            for k in range(4):
                if (k, g) in after:
                    pl.when(i == k)(lambda work=after[k, g]: (work(), None)[1])
        return 0

    lax.fori_loop(0, 4, attention_pass, 0)
    finish(3)
    exchange(1)
    turns = ((0, 0, 2), (1, 0, 1), (0, 2, 3), (1, 1, 2), (0, 3, 4), (1, 2, 4))
    exchanged(0)
    for k, turn in enumerate(turns):
        if k == 1:
            exchanged(1)
        project_out(*turn)
    for turn in turns:
        sum_up(*turn)

    own_rows = zl

    def final_step(slot, _):
        await_recv(zgot.at[slot], z_recv.at[slot])
        cols = pl.ds(pl.multiple_of(slot * width, width), width)
        out_ref[:, cols] = (mine[own_rows, slot] + zgot[slot].astype(F32)).astype(BF16)
        return 0

    lax.fori_loop(0, 2 * steps, final_step, 0)

    for copy in sends:
        copy.wait_send()

    def await_send(src, ssem):
        pltpu.make_async_remote_copy(
            src_ref=src, dst_ref=src, send_sem=ssem, recv_sem=ssem,
            device_id=(me, head), device_id_type=MESH,
        ).wait_send()

    for i in range(1, N_CTX):
        target = (me + i) % N_CTX
        await_send(kv_stage.at[target], kva_send.at[target])
        await_send(q_stage.at[target], qa_send.at[target])

    def drain_kv(q, _):
        def sent(src, way):
            place = place_of(*src)
            await_send(kv.at[q, place], kv_send.at[q, place, way])

        for way in range(4):
            sent((0, 0, 0), way)
        for way in range(1, 4):
            sent((1, 0, 0), way)
        for dz in range(2):
            for dx in range(1, 4):
                sent((dz, dx, 0), 3)
        sent((0, 3, 0), 1)
        sent((1, 1, 0), 2)
        return 0

    lax.fori_loop(0, 4, drain_kv, 0)
    await_send(wo_a.at[half, :], wc_send.at[0])
    await_send(wo_b.at[half, :], wc_send.at[1])

    def drain(c, _):
        for z in range(2):
            await_send(part_a.at[z, c], part_send.at[z, 0, c])
            await_send(part_b.at[z, c], part_send.at[z, 1, c])
            await_send(att.at[0, 0], att_send.at[z, c])
        await_send(zsend.at[c], z_send.at[c])
        await_send(zsend.at[steps + c], z_send.at[steps + c])
        return 0

    lax.fori_loop(0, steps, drain, 0)


def body(hidden_states, norm_gain, query_weight, key_weight, value_weight, output_weight, keep_flags, span_order):
    base, inner = rope_tables()
    vmem = pl.BlockSpec(memory_space=pltpu.VMEM)
    smem = pl.BlockSpec(memory_space=pltpu.SMEM)
    anywhere = pl.BlockSpec(memory_space=pl.ANY)
    dma = pltpu.SemaphoreType.DMA
    return pl.pallas_call(
        kernel,
        out_shape=jax.ShapeDtypeStruct((64, 4096), BF16),
        in_specs=[anywhere, vmem, anywhere, anywhere, anywhere, anywhere, smem, smem, anywhere, vmem],
        out_specs=vmem,
        scratch_shapes=[
            pltpu.VMEM((32, 32, 4096), BF16),
            pltpu.VMEM((4096, 512), BF16),
            pltpu.VMEM((4096, 256), BF16),
            pltpu.VMEM((512, 4096), BF16),
            pltpu.VMEM((512, 2048), BF16),
            pltpu.VMEM((512, 2048), BF16),
            pltpu.VMEM((32, 2, 1, 128), F32),
            pltpu.VMEM((32, 32, 4096), BF16),
            pltpu.VMEM((1, 128), jnp.int32),
            pltpu.VMEM((16, 1, 128), jnp.int32),
            pltpu.SMEM((16, 1, 128), jnp.int32),
            pltpu.VMEM((32, 2, 32, 128), BF16),
            pltpu.VMEM((32, 4, 32, 128), BF16),
            pltpu.VMEM((16, 2, 2, 32, 128), BF16),
            pltpu.VMEM((16, 2, 4, 32, 128), BF16),
            pltpu.VMEM((16, 2, 2, 32, 128), BF16),
            pltpu.VMEM((16, 2, 4, 32, 128), BF16),
            pltpu.VMEM((2048, 128), BF16),
            pltpu.VMEM((4, 16, 2, 128, 128), BF16),
            pltpu.VMEM((2048, 256), F32),
            pltpu.VMEM((2048, 128), F32),
            pltpu.VMEM((4, 2, 64, 512), BF16),
            pltpu.VMEM((2, 2, 64, 512), BF16),
            pltpu.VMEM((2, 2, 64, 512), BF16),
            pltpu.VMEM((2, 4, 64, 512), BF16),
            pltpu.VMEM((2, 4, 64, 512), BF16),
            pltpu.VMEM((2, 4, 64, 512), BF16),
            pltpu.VMEM((2, 4, 64, 512), BF16),
            pltpu.VMEM((2, 8, 64, 512), F32),
            pltpu.VMEM((8, 64, 512), BF16),
            pltpu.VMEM((8, 64, 512), BF16),
            dma((4,)),
            dma((8,)),
            dma((16,)), dma((16,)),
            dma((16,)), dma((16,)),
            dma((16,)), dma((16,)),
            dma((4, 16, 4)), dma((4, 16)),
            dma((2,)), dma((2,)), dma((2,)), dma((2,)),
            dma((2, 4)), dma((2, 4)),
            dma((2, 2, 4)), dma((2, 2, 4)),
            dma((8,)), dma((8,)),
            dma,
        ],
        compiler_params=pltpu.CompilerParams(
            collective_id=1, has_side_effects=True, vmem_limit_bytes=60 * 2**20
        ),
        name="prefill",
    )(
        hidden_states.reshape(32, 32, 4096), norm_gain.reshape(1, 4096), query_weight, key_weight, value_weight, output_weight,
        keep_flags, span_order, jnp.asarray(base), jnp.asarray(inner),
    )


def solution(mesh):
    return jax.shard_map(
        body,
        mesh=mesh,
        in_specs=(
            P("ctx", None),
            P(),
            P(None, "head"),
            P(None, "head"),
            P(None, "head"),
            P("head", None),
            P("ctx"),
            P(),
        ),
        out_specs=P(("ctx", "head"), None),
        check_vma=False,
    )
```
